1024 devices in a mesh: az: 256 (over y, x_lo, z), ht: 4 (over x_hi, core).
Axes of the slice: x: 4 (x_hi: 2, x_lo: 2; x = x_hi * 2 + x_lo), y: 4, z: 32, core: 2. Of those that a mesh axis runs over, the one named last changes fastest.
Arguments:
- right_side: float32 [64, 3072, 256], P('ht', 'az'), may hold values from -6 to 6
- base_coef: float32 [64, 3072, 256], P('ht', 'az'), may hold values from 0.3 to 3
- cell_type: int32 [64, 3072, 256], P('ht', 'az'), may hold values from 0 to 2
Outputs:
- pressure: float32 [64, 3072, 256], P('ht', 'az')
The draws below stay inside these ranges and needn't reach their ends.
All inputs are finite; a program needn't handle non-finite values.
Results may differ from the reference program's by a relative error of at most 0.00002.
Values sent between devices are 32-bit elements; how exact they have to be, the bound alone decides.
A program may use at most 64 MiB of HBM per device.

```python
import math
import jax
import jax.numpy as jnp

NR = 256
DEGREE = 4
COARSE_SWEEPS = 6
NA = 3072
NH = 64


def with_ends(values, own_key, low, high):
    extent = values.shape
    index_at = [jax.random.randint(jax.random.fold_in(own_key, axis), (), 0, extent[axis]) for axis in range(len(extent))]
    values = values.at[tuple(index_at)].set(low)
    longest = extent.index(max(extent))
    index_at[longest] = (index_at[longest] + 1) % extent[longest]
    return values.at[tuple(index_at)].set(high)


def block_levels(key, dims, shards, smallest, high):
    def one(position, parts):
        draws = jax.random.uniform(jax.random.fold_in(jax.random.fold_in(key, 6), position), (parts,), jnp.float32, smallest / len(shards), high / len(shards))
        return jnp.repeat(jnp.exp(draws), dims[position] // parts).reshape((-1,) + (1,) * (len(dims) - position - 1))

    factor_of = one(*shards[0])
    for cut in shards[1:]:
        factor_of = factor_of * one(*cut)
    return factor_of


def bell_draw(rng, shape, width, reach, split=(), kind=jnp.bfloat16):
    loudness = block_levels(rng, shape, split, -0.22, 0.18) if split else 1.0
    values = jax.random.normal(rng, shape, jnp.float32) * width * loudness
    return jnp.minimum(jnp.maximum(values, -reach), reach).astype(kind)


def setup_inputs(seed: int = 0) -> dict:
    seeds = jax.random.split(jax.random.key(seed), 4)
    right_side = bell_draw(seeds[0], (NH, NA, NR), 1.0, 6.0, ((0, 4), (1, 256)), jnp.float32)
    base_coef = jnp.clip(jnp.exp(math.log(3.0) - 2.3025851 * jax.random.uniform(seeds[1], (NH, NA, NR), jnp.float32) ** block_levels(seeds[1], (NH, NA, NR), ((0, 4), (1, 256)), -0.2, 0.2)), 0.3, 3.0)
    cell_type = with_ends(jax.random.randint(seeds[2], (NH, NA, NR), 0, 3), jax.random.fold_in(seeds[2], 1), 0, 2).astype(jnp.int32)
    return {"right_side": right_side, "base_coef": base_coef, "cell_type": cell_type}


shift_value = 0.002
smooth_low = 0.3
coarse_low = 0.02
high_end = 2.0


def conductivity(base_coef, cell_type):
    factor = jnp.where(cell_type == 0, 0.1, jnp.where(cell_type == 1, 0.4, 1.0)).astype(jnp.float32)
    return base_coef * factor


def neighbours(values, coeffs):
    centre = values[1:-1, 1:-1]
    centre_coef = coeffs[1:-1, 1:-1]
    padded_field = jnp.pad(centre, ((0, 0), (0, 0), (1, 1)))
    padded_coef = jnp.pad(centre_coef, ((0, 0), (0, 0), (1, 1)))
    pairs = [(values[2:, 1:-1], coeffs[2:, 1:-1]), (values[:-2, 1:-1], coeffs[:-2, 1:-1]),
             (values[1:-1, 2:], coeffs[1:-1, 2:]), (values[1:-1, :-2], coeffs[1:-1, :-2]),
             (padded_field[:, :, 2:], padded_coef[:, :, 2:]), (padded_field[:, :, :-2], padded_coef[:, :, :-2])]
    return centre, centre_coef, pairs


def stencil(values, coeffs, spacing):
    centre, centre_coef, pairs = neighbours(values, coeffs)
    fluxes = jnp.zeros_like(centre)
    for value_next, coef_next in pairs:
        fluxes = fluxes + 0.5 * (centre_coef + coef_next) * (centre - value_next)
    return shift_value * centre + spacing * fluxes


def diagonal(coeffs, spacing):
    centre, centre_coef, pairs = neighbours(coeffs, coeffs)
    total = jnp.zeros_like(centre)
    for value_next, coef_next in pairs:
        total = total + 0.5 * (centre_coef + coef_next)
    return shift_value + spacing * total


def same(array):
    return array


def chebyshev(source, coeffs, pivots, inside, apply_op, shrink, degree, low_end, want_res):
    middle = 0.5 * (high_end + low_end)
    spread = 0.5 * (high_end - low_end)
    sigma_ratio = middle / spread
    rho_now = 1.0 / sigma_ratio
    direction = inside * source / pivots / middle
    iterate = direction
    for sweep_index in range(degree - 1):
        image = apply_op(iterate, coeffs)
        iterate, direction, source = shrink(iterate), shrink(direction), shrink(source)
        coeffs, pivots, inside = shrink(coeffs), shrink(pivots), shrink(inside)
        rho_next = 1.0 / (2.0 * sigma_ratio - rho_now)
        direction = inside * (rho_next * rho_now * direction + (2.0 * rho_next / spread) * (source - image) / pivots)
        iterate = iterate + direction
        rho_now = rho_next
    residual = None
    if want_res:
        image = apply_op(iterate, coeffs)
        iterate = shrink(iterate)
        residual = shrink(source) - image
    return iterate, residual


def restrict(values):
    shape = values.shape
    blocks = values.reshape(shape[0] // 2, 2, shape[1] // 2, 2, shape[2] // 2, 2)
    return blocks.mean(axis=(1, 3, 5))


def prolong(values):
    return jnp.repeat(jnp.repeat(jnp.repeat(values, 2, 0), 2, 1), 2, 2)


def ref_extend(values):
    wrapped = jnp.concatenate([values[:, -1:], values, values[:, :1]], axis=1)
    return jnp.pad(wrapped, ((1, 1), (0, 0), (0, 0)))


def solve_level(source, coeffs, spacing, degree, low_end, want_res):
    coef_ext = ref_extend(coeffs)
    pivots = diagonal(coef_ext, spacing)

    def apply_op(iterate, coef_now):
        return stencil(ref_extend(iterate), coef_now, spacing)

    return chebyshev(source, coef_ext, pivots, 1.0, apply_op, same, degree, low_end, want_res)


def reference(right_side, base_coef, cell_type):
    kappa_fine = conductivity(base_coef, cell_type)
    fine_x, fine_r = solve_level(right_side, kappa_fine, 1.0, DEGREE, smooth_low, True)
    middle_b = restrict(fine_r)
    kappa_mid = restrict(kappa_fine)
    middle_x, middle_r = solve_level(middle_b, kappa_mid, 0.25, DEGREE, smooth_low, True)
    coarse_b = restrict(middle_r)
    kappa_coarse = restrict(kappa_mid)
    coarse_x, unused = solve_level(coarse_b, kappa_coarse, 0.0625, COARSE_SWEEPS, coarse_low, False)
    return fine_x + prolong(middle_x + prolong(coarse_x))
```

```python
import functools

import jax
import jax.numpy as jnp
from jax import lax
from jax.experimental import pallas as pl
from jax.experimental.pallas import tpu as pltpu
from jax.sharding import PartitionSpec as P

DEGREE = 4
COARSE_SWEEPS = 6

shift_value = 0.002
smooth_low = 0.3
coarse_low = 0.02
high_end = 2.0

F32 = jnp.float32
BF16 = jnp.bfloat16
MESH = pl.DeviceIdType.MESH

SIDES = [(0, 1), (0, -1)]
ENDS = [(1, 0), (-1, 0)]
CORNERS = [(1, 1), (1, -1), (-1, 1), (-1, -1)]
NEAR = SIDES + ENDS + CORNERS
REACH = 2


def chebyshev_steps(degree, low_end):
    middle = 0.5 * (high_end + low_end)
    spread = 0.5 * (high_end - low_end)
    sigma_ratio = middle / spread
    rho_now = 1.0 / sigma_ratio
    steps = []
    for _ in range(degree - 1):
        rho_next = 1.0 / (2.0 * sigma_ratio - rho_now)
        steps.append((rho_next * rho_now, 2.0 * rho_next / spread))
        rho_now = rho_next
    return 1.0 / middle, steps


def exact_dot(values, weights):
    high = values.astype(BF16)
    rest = values - high.astype(F32)
    mid = rest.astype(BF16)
    low = (rest - mid.astype(F32)).astype(BF16)
    total = jnp.dot(high, weights, preferred_element_type=F32)
    total = total + jnp.dot(mid, weights, preferred_element_type=F32)
    return total + jnp.dot(low, weights, preferred_element_type=F32)


def each_row(start, count, block, body):
    def step(i, carry):
        for j in range(block):
            body(start + i * block + j)
        return carry

    lax.fori_loop(0, count // block, step, 0)


def next_in(values, axis):
    return pltpu.roll(values, values.shape[axis] - 1, axis)


def last_in(values, axis):
    return pltpu.roll(values, 1, axis)


def face_coefs(k, low, high, half, last_lane, first_lane):
    up = half * (k + high)
    down = half * (k + low)
    side = half * (k + next_in(k, 0))
    out = half * (k + jnp.where(last_lane, 0.0, next_in(k, 1)))
    back = jnp.where(first_lane, half * k, last_in(out, 1))
    pivots = shift_value + (up + down + side + last_in(side, 0) + out + back)
    return up, down, side, jnp.where(last_lane, 0.0, out), pivots


def in_layer(x, side, out):
    return (
        side * next_in(x, 0) + last_in(side * x, 0) + out * next_in(x, 1) + last_in(out * x, 1)
    )


class Level:
    def __init__(self, refs, spacing, low_end, degree):
        self.k, self.b, self.x, self.y, self.d, self.up, self.side, self.out, self.inv, self.piv = refs
        self.rows, self.sub, self.lanes = self.b.shape
        self.half = 0.5 * spacing
        self.first, self.steps = chebyshev_steps(degree, low_end)

    def set_up(self, begin, end, block):
        lane = lax.broadcasted_iota(jnp.int32, (self.sub, self.lanes), 1)
        last_lane, first_lane = lane == self.lanes - 1, lane == 0

        def body(h):
            up, _, side, out, piv = face_coefs(
                self.k[h + 1], self.k[h], self.k[h + 2], self.half, last_lane, first_lane
            )
            self.up[h], self.side[h], self.out[h], self.piv[h] = up, side, out, piv
            inside = jnp.where((h >= begin) & (h < end), 1.0, 0.0).astype(F32)
            self.inv[h] = inside / piv

        each_row(0, self.rows, block, body)

    def gathered(self, h):
        x = self.x[h]
        total = self.b[h] + self.up[h] * self.x[h + 1] + self.up[h - 1] * self.x[h - 1]
        return total + in_layer(x, self.side[h], self.out[h]), x

    def smooth(self, block):
        def start(h):
            self.x[h] = self.b[h] * self.inv[h] * self.first

        each_row(0, self.rows, block, start)
        for number, (keep, add) in enumerate(self.steps):

            def body(h):
                total, x = self.gathered(h)
                d = keep * (self.d[h] if number else x) + add * (total * self.inv[h] - x)
                self.d[h] = d
                self.y[h] = x + d

            each_row(number + 1, self.rows - 2 * (number + 1), block, body)
            self.x, self.y = self.y, self.x

    def residual(self, h):
        total, x = self.gathered(h)
        return total - self.piv[h] * x


def kernel(n_ht, n_az, rhs_hbm, coef_hbm, type_hbm, res_hbm, s):
    ht, az = lax.axis_index("ht"), lax.axis_index("az")
    has = {1: ht < n_ht - 1, -1: ht > 0}
    rows, cols, _ = rhs_hbm.shape

    def device(dh, da):
        return {"ht": ht + dh, "az": lax.rem(az + (da + n_az), n_az)}

    def there(dh, run):
        if dh == 0:
            run()
        else:
            pl.when(has[dh])(run)

    loads = [
        pltpu.make_async_copy(src, dst, s.load_sem.at[i])
        for i, (src, dst) in enumerate(
            [(coef_hbm, s.coef), (type_hbm, s.kind), (rhs_hbm, s.rhs)]
        )
    ]
    for load in loads:
        load.start()

    barrier = pltpu.get_barrier_semaphore()
    far = [
        (dh, da)
        for da in range(-REACH, REACH + 1)
        for dh in range(n_ht)
        if (dh, da) != (0, 0)
    ]

    def far_device(dh, da):
        return {"ht": lax.rem(ht + dh, n_ht), "az": lax.rem(az + (da + n_az), n_az)}

    for dh, da in far:
        pl.semaphore_signal(barrier, inc=1, device_id=far_device(dh, da), device_id_type=MESH)

    sent = []

    def copies(first_slot, directions, src, dst):
        made = []
        for i, (dh, da) in enumerate(directions):
            slot = first_slot + i
            copy = pltpu.make_async_remote_copy(
                src_ref=src(dh, da),
                dst_ref=dst(dh, da),
                send_sem=s.send_sem.at[slot],
                recv_sem=s.recv_sem.at[slot],
                device_id=device(dh, da),
                device_id_type=MESH,
            )
            there(dh, copy.start)
            made.append((dh, da, copy))
        sent.extend(made)
        return {(dh, da): copy for dh, da, copy in made}

    s.k0[...] = jnp.zeros_like(s.k0)
    s.b0[...] = jnp.zeros_like(s.b0)
    s.k1[...] = jnp.zeros_like(s.k1)
    s.b1[...] = jnp.zeros_like(s.b1)
    s.k2[...] = jnp.zeros_like(s.k2)
    s.b2[...] = jnp.zeros_like(s.b2)
    s.x2[...] = jnp.zeros_like(s.x2)
    s.y2[...] = jnp.zeros_like(s.y2)

    def iotas(shape):
        return lax.broadcasted_iota(jnp.int32, shape, 0), lax.broadcasted_iota(jnp.int32, shape, 1)

    def as_weights(picked, value):
        return jnp.where(picked, value, 0.0).astype(BF16)

    i, j = iotas(s.down0.shape)
    s.down0[...] = as_weights(i // 2 == j, 0.125)
    i, j = iotas(s.down1.shape)
    s.down1[...] = as_weights(i // 2 == j % 64, 0.125)
    i, j = iotas(s.wide1.shape)
    s.wide1[...] = as_weights(i == j // 2, 1.0)
    i, j = iotas(s.wide2a.shape)
    s.wide2a[...] = as_weights(i == j // 2, 1.0)
    s.wide2b[...] = as_weights(i == 64 + j // 2, 1.0)

    loads[0].wait()
    loads[1].wait()

    def conductivity(h):
        kind = s.kind[h]
        factor = jnp.where(kind == 0, 0.1, jnp.where(kind == 1, 0.4, 1.0)).astype(F32)
        kappa = s.coef[h] * factor
        s.kappa[h] = kappa
        s.k0[h + 5, 0:cols] = kappa
        s.k4_out[0, h] = kappa[cols - 4 : cols]
        s.k4_out[1, h] = kappa[0:4]
        s.k5_out[0, h] = kappa[cols - 5 : cols - 4]
        s.k5_out[1, h] = kappa[4:5]

    each_row(0, rows, 4, conductivity)
    pl.semaphore_wait(barrier, len(far))

    def pick(ref, dh, da, layers, size):
        side = 0 if da == 1 else 1
        if dh == 0:
            return ref.at[side]
        return ref.at[side, size - layers : size] if dh == 1 else ref.at[side, 0:layers]

    def layers_of(ref, dh, layers):
        size = ref.shape[0]
        return ref.at[size - layers : size] if dh == 1 else ref.at[0:layers]

    def end(dh):
        return 0 if dh == 1 else 1

    def corner(dh, da):
        return (0 if dh == 1 else 2) + (0 if da == 1 else 1)

    k4 = copies(0, SIDES, lambda dh, da: pick(s.k4_out, dh, da, 0, 0), lambda dh, da: s.k4_in.at[0 if da == 1 else 1])
    k5 = copies(2, SIDES, lambda dh, da: pick(s.k5_out, dh, da, 0, 0), lambda dh, da: s.k5_in.at[0 if da == 1 else 1])
    ke = copies(4, ENDS, lambda dh, da: layers_of(s.kappa, dh, 5), lambda dh, da: s.ke_in.at[end(dh)])
    kc = copies(6, CORNERS, lambda dh, da: pick(s.k4_out, dh, da, 4, rows), lambda dh, da: s.kc_in.at[corner(dh, da)])

    loads[2].wait()

    def source(h):
        rhs = s.rhs[h]
        s.b0[h + 4, 0:cols] = rhs
        s.b4_out[0, h] = rhs[cols - 4 : cols]
        s.b4_out[1, h] = rhs[0:4]

    each_row(0, rows, 4, source)
    b4 = copies(10, SIDES, lambda dh, da: pick(s.b4_out, dh, da, 0, 0), lambda dh, da: s.b4_in.at[0 if da == 1 else 1])
    be = copies(12, ENDS, lambda dh, da: layers_of(s.rhs, dh, 4), lambda dh, da: s.be_in.at[end(dh)])
    bc = copies(14, CORNERS, lambda dh, da: pick(s.b4_out, dh, da, 3, rows), lambda dh, da: s.bc_in.at[corner(dh, da)])

    mid_rows, mid_cols = rows // 2, cols // 2

    def restrict0(pair_sum):
        each_row(0, mid_rows, 4, pair_sum)
        s.halves[...] = exact_dot(s.pairs[...].reshape(mid_rows * 16, -1), s.down0[...])
        count = mid_rows * 8
        means = s.halves[pl.ds(0, count, stride=2), :] + s.halves[pl.ds(1, count, stride=2), :]
        return means.reshape(mid_rows, 8, -1)

    def restrict1(values):
        parts = [values[2 * i] + values[2 * i + 1] for i in range(mid_rows // 2)]
        s.quarters[...] = exact_dot(jnp.concatenate(parts, axis=0), s.down1[...])
        means = s.quarters[pl.ds(0, 16, stride=2), :] + s.quarters[pl.ds(1, 16, stride=2), :]
        lane = lax.broadcasted_iota(jnp.int32, (8, 128), 1)
        return jnp.where(lane < 64, means[0:8], means[8:16])

    def pair_of_kappa(i):
        s.pairs[i, 0:cols] = s.kappa[2 * i] + s.kappa[2 * i + 1]

    s.pairs[...] = jnp.zeros_like(s.pairs)
    kappa1 = restrict0(pair_of_kappa)
    s.kappa1[...] = kappa1
    s.k1[5 : 5 + mid_rows, 0:mid_cols] = kappa1[:, 0:mid_cols]
    m4 = copies(18, SIDES, lambda dh, da: s.kappa1, lambda dh, da: s.m4_in.at[0 if da == 1 else 1])
    me = copies(20, ENDS, lambda dh, da: layers_of(s.kappa1, dh, 5), lambda dh, da: s.me_in.at[end(dh)])
    mc = copies(22, CORNERS, lambda dh, da: layers_of(s.kappa1, dh, 4), lambda dh, da: s.mc_in.at[corner(dh, da)])

    def spread(packed, blocks, send_sem, recv_sem, kept):
        kept[...] = packed
        made = []
        for dh, da in far:
            copy = pltpu.make_async_remote_copy(
                src_ref=kept,
                dst_ref=blocks.at[(REACH - da) * n_ht + ht],
                send_sem=send_sem,
                recv_sem=recv_sem,
                device_id=far_device(dh, da),
                device_id_type=MESH,
            )
            copy.start()
        blocks[REACH * n_ht + ht] = packed

    def all_of(blocks, sem):
        some = blocks.at[0 : len(far)]
        return pltpu.make_async_copy(some, some, sem)

    spread(restrict1(kappa1), s.k2_blocks, s.far_send.at[0], s.far_recv.at[0], s.kappa2)

    def arrived(made, place):
        for (dh, da), copy in made.items():

            def take(dh=dh, da=da, copy=copy):
                copy.wait_recv()
                place(dh, da)

            there(-dh, take)

    def height(dh, layers, halo, size):
        return slice(halo - layers, halo) if dh == 1 else slice(halo + size, halo + size + layers)

    def place_k4(dh, da):
        low = 20 if da == 1 else cols
        s.k0[5 : 5 + rows, low : low + 4] = s.k4_in[0 if da == 1 else 1]

    def place_k5(dh, da):
        low = 19 if da == 1 else cols + 4
        s.k0[5 : 5 + rows, low : low + 1] = s.k5_in[0 if da == 1 else 1]

    def place_ke(dh, da):
        s.k0[height(dh, 5, 5, rows), 0:cols] = s.ke_in[end(dh)]

    def place_kc(dh, da):
        low = 20 if da == 1 else cols
        s.k0[height(dh, 4, 5, rows), low : low + 4] = s.kc_in[corner(dh, da)]

    arrived(k4, place_k4)
    arrived(k5, place_k5)
    arrived(ke, place_ke)
    arrived(kc, place_kc)

    fine = Level((s.k0, s.b0, s.x0, s.y0, s.d0, s.up0, s.side0, s.out0, s.inv0, s.piv0), 1.0, smooth_low, DEGREE)
    fine.set_up(jnp.where(has[-1], 0, 4), jnp.where(has[1], rows + 8, rows + 4), 2)

    def place_b4(dh, da):
        low = 20 if da == 1 else cols
        s.b0[4 : 4 + rows, low : low + 4] = s.b4_in[0 if da == 1 else 1]

    def place_be(dh, da):
        s.b0[height(dh, 4, 4, rows), 0:cols] = s.be_in[end(dh)]

    def place_bc(dh, da):
        low = 20 if da == 1 else cols
        s.b0[height(dh, 3, 4, rows), low : low + 4] = s.bc_in[corner(dh, da)]

    arrived(b4, place_b4)
    arrived(be, place_be)
    arrived(bc, place_bc)
    fine.smooth(2)

    def pair_of_residual(i):
        pair = fine.residual(4 + 2 * i) + fine.residual(5 + 2 * i)
        s.pairs[i] = pair[0:16]

    b1 = restrict0(pair_of_residual)
    s.source1[...] = b1
    s.b1[4 : 4 + mid_rows, 0:mid_cols] = b1[:, 0:mid_cols]
    s.n4_out[0] = b1[:, mid_cols - 4 : mid_cols]
    s.n4_out[1] = b1[:, 0:4]
    n4 = copies(26, SIDES, lambda dh, da: pick(s.n4_out, dh, da, 0, 0), lambda dh, da: s.n4_in.at[0 if da == 1 else 1])
    ne = copies(28, ENDS, lambda dh, da: layers_of(s.source1, dh, 4), lambda dh, da: s.ne_in.at[end(dh)])
    nc = copies(30, CORNERS, lambda dh, da: pick(s.n4_out, dh, da, 3, mid_rows), lambda dh, da: s.nc_in.at[corner(dh, da)])

    def place_m4(dh, da):
        if da == 1:
            s.k1[5 : 5 + mid_rows, 11:16] = s.m4_in[0, :, mid_cols - 5 : mid_cols]
        else:
            s.k1[5 : 5 + mid_rows, 6:11] = s.m4_in[1, :, 0:5]

    def place_me(dh, da):
        s.k1[height(dh, 5, 5, mid_rows), 0:mid_cols] = s.me_in[end(dh), :, 0:mid_cols]

    def place_mc(dh, da):
        here = s.mc_in[corner(dh, da)]
        if da == 1:
            s.k1[height(dh, 4, 5, mid_rows), 12:16] = here[:, mid_cols - 4 : mid_cols]
        else:
            s.k1[height(dh, 4, 5, mid_rows), 6:10] = here[:, 0:4]

    arrived(m4, place_m4)
    arrived(me, place_me)
    arrived(mc, place_mc)
    middle = Level((s.k1, s.b1, s.x1, s.y1, s.d1, s.up1, s.side1, s.out1, s.inv1, s.piv1), 0.25, smooth_low, DEGREE)
    middle.set_up(jnp.where(has[-1], 0, 4), jnp.where(has[1], mid_rows + 8, mid_rows + 4), 4)

    def place_n4(dh, da):
        low = 12 if da == 1 else mid_cols
        s.b1[4 : 4 + mid_rows, low : low + 4] = s.n4_in[0 if da == 1 else 1]

    def place_ne(dh, da):
        s.b1[height(dh, 4, 4, mid_rows), 0:mid_cols] = s.ne_in[end(dh), :, 0:mid_cols]

    def place_nc(dh, da):
        low = 12 if da == 1 else mid_cols
        s.b1[height(dh, 3, 4, mid_rows), low : low + 4] = s.nc_in[corner(dh, da)]

    arrived(n4, place_n4)
    arrived(ne, place_ne)
    arrived(nc, place_nc)
    middle.smooth(2)
    r1 = [middle.residual(4 + i)[0:8] for i in range(mid_rows)]
    spread(restrict1(r1), s.b2_blocks, s.far_send.at[1], s.far_recv.at[1], s.source2)

    coarse_cols = mid_cols // 2

    def lay_out(blocks, field):
        for step in range(-REACH, REACH + 1):
            low = (step * coarse_cols + 16) % 16
            for t in range(n_ht):
                block = blocks[(REACH + step) * n_ht + t]
                field[1 + 2 * t, low : low + coarse_cols] = block[0:coarse_cols]
                field[2 + 2 * t, low : low + coarse_cols] = block[4 : 4 + coarse_cols]

    lane = lax.broadcasted_iota(jnp.int32, (16, 128), 1)
    front = lane < 64
    last_lane, first_lane = lane % 64 == 63, lane % 64 == 0

    def above(field, row, i):
        if i == 0:
            return field[row + 1]
        return pltpu.roll(jnp.where(front, field[row + 1], field[row - 1]), 64, 1)

    def below(field, row, i):
        if i == 1:
            return field[row - 1]
        return pltpu.roll(jnp.where(front, field[row + 1], field[row - 1]), 64, 1)

    all_of(s.k2_blocks, s.far_recv.at[0]).wait()
    lay_out(s.k2_blocks, s.k2)

    first, steps = chebyshev_steps(COARSE_SWEEPS, coarse_low)

    def coarse_set_up(t):
        for i in range(2):
            row = 1 + 2 * t + i
            up, down, side, out, piv = face_coefs(
                s.k2[row], below(s.k2, row, i), above(s.k2, row, i), 0.5 * 0.0625, last_lane, first_lane
            )
            s.up2[row], s.down2[row], s.side2[row], s.out2[row] = up, down, side, out
            s.inv2[row] = 1.0 / piv

    each_row(0, n_ht, 2, coarse_set_up)

    all_of(s.b2_blocks, s.far_recv.at[1]).wait()
    lay_out(s.b2_blocks, s.b2)

    for row in range(1, 1 + 2 * n_ht):
        s.x2[row] = s.b2[row] * s.inv2[row] * first
    x2, y2 = s.x2, s.y2
    for number, (keep, add) in enumerate(steps):

        def sweep(t):
            for i in range(2):
                row = 1 + 2 * t + i
                x = x2[row]
                total = s.b2[row] + s.up2[row] * above(x2, row, i) + s.down2[row] * below(x2, row, i)
                total = total + in_layer(x, s.side2[row], s.out2[row])
                d = keep * (s.d2[row] if number else x) + add * (total * s.inv2[row] - x)
                s.d2[row] = d
                y2[row] = x + d

        if number < len(steps) - 1:
            each_row(0, n_ht, 4, sweep)
        else:
            sweep(ht)
        x2, y2 = y2, x2

    own = jnp.concatenate([x2[1 + 2 * ht, 0:8], x2[2 + 2 * ht, 0:8]], axis=0)
    spread_out = [exact_dot(own, s.wide2a[...]), exact_dot(own, s.wide2b[...])]
    for h in range(mid_rows // 2):
        part = spread_out[h // 2][8 * (h % 2) : 8 * (h % 2) + 4]
        s.raised1[pl.ds(h * 8, 4, stride=2), :] = part
        s.raised1[pl.ds(h * 8 + 1, 4, stride=2), :] = part
    for h in range(mid_rows):
        part = middle.x[4 + h, 0:8] + s.raised1[(h // 2) * 8 : (h // 2) * 8 + 8]
        s.raised0[pl.ds(h * 16, 8, stride=2), :] = part
        s.raised0[pl.ds(h * 16 + 1, 8, stride=2), :] = part
    raised = exact_dot(s.raised0[...], s.wide1[...]).reshape(mid_rows, 16, -1)
    for h in range(mid_rows):
        part = raised[h, 0:cols]
        s.res[2 * h] = fine.x[4 + 2 * h, 0:cols] + part
        s.res[2 * h + 1] = fine.x[5 + 2 * h, 0:cols] + part
    store = pltpu.make_async_copy(s.res, res_hbm, s.load_sem.at[3])
    store.start()

    for dh, da, copy in sent:
        there(dh, copy.wait_send)
    all_of(s.k2_blocks, s.far_send.at[0]).wait()
    all_of(s.b2_blocks, s.far_send.at[1]).wait()
    store.wait()


class Scratch:
    pass


def scratch_shapes(rows, cols, lanes, n_ht):
    mid_rows, mid_lanes = rows // 2, lanes // 2
    blocks = (2 * REACH + 1) * n_ht
    fields = {
        "coef": (rows, cols, lanes),
        "rhs": (rows, cols, lanes),
        "kappa": (rows, cols, lanes),
        "res": (rows, cols, lanes),
        "k4_out": (2, rows, 4, lanes),
        "k4_in": (2, rows, 4, lanes),
        "k5_out": (2, rows, 1, lanes),
        "k5_in": (2, rows, 1, lanes),
        "ke_in": (2, 5, cols, lanes),
        "kc_in": (4, 4, 4, lanes),
        "b4_out": (2, rows, 4, lanes),
        "b4_in": (2, rows, 4, lanes),
        "be_in": (2, 4, cols, lanes),
        "bc_in": (4, 3, 4, lanes),
        "pairs": (mid_rows, 16, lanes),
        "halves": (mid_rows * 16, mid_lanes),
        "quarters": (mid_rows // 2 * 8, mid_lanes),
        "kappa1": (mid_rows, 8, mid_lanes),
        "m4_in": (2, mid_rows, 8, mid_lanes),
        "me_in": (2, 5, 8, mid_lanes),
        "mc_in": (4, 4, 8, mid_lanes),
        "source1": (mid_rows, 8, mid_lanes),
        "n4_out": (2, mid_rows, 4, mid_lanes),
        "n4_in": (2, mid_rows, 4, mid_lanes),
        "ne_in": (2, 4, 8, mid_lanes),
        "nc_in": (4, 3, 4, mid_lanes),
        "kappa2": (8, 128),
        "source2": (8, 128),
        "k2_blocks": (blocks, 8, 128),
        "b2_blocks": (blocks, 8, 128),
        "raised1": (mid_rows // 2 * 8, mid_lanes),
        "raised0": (mid_rows * 16, mid_lanes),
    }
    for level, (size, sub, width) in enumerate(
        [(rows, 24, lanes), (mid_rows, 16, mid_lanes), (2 * n_ht - 6, 16, 128)]
    ):
        fields[f"k{level}"] = (size + 10, sub, width)
        for name in ("b", "x", "y", "d", "up", "down", "side", "out", "inv", "piv"):
            fields[f"{name}{level}"] = (size + 8, sub, width)
    shapes = {name: pltpu.VMEM(shape, F32) for name, shape in fields.items()}
    shapes["kind"] = pltpu.VMEM((rows, cols, lanes), jnp.int32)
    shapes["down0"] = pltpu.VMEM((lanes, mid_lanes), BF16)
    shapes["down1"] = pltpu.VMEM((mid_lanes, 128), BF16)
    shapes["wide1"] = pltpu.VMEM((mid_lanes, lanes), BF16)
    shapes["wide2a"] = pltpu.VMEM((128, mid_lanes), BF16)
    shapes["wide2b"] = pltpu.VMEM((128, mid_lanes), BF16)
    shapes["load_sem"] = pltpu.SemaphoreType.DMA((4,))
    shapes["send_sem"] = pltpu.SemaphoreType.DMA((34,))
    shapes["recv_sem"] = pltpu.SemaphoreType.DMA((34,))
    shapes["far_send"] = pltpu.SemaphoreType.DMA((2,))
    shapes["far_recv"] = pltpu.SemaphoreType.DMA((2,))
    return shapes


def solution(mesh):
    n_ht, n_az = mesh.shape["ht"], mesh.shape["az"]

    def on_device(right_side, base_coef, cell_type):
        shapes = scratch_shapes(*right_side.shape, n_ht)

        def body(rhs, coef, kind, res, *refs):
            s = Scratch()
            for name, ref in zip(shapes, refs):
                setattr(s, name, ref)
            kernel(n_ht, n_az, rhs, coef, kind, res, s)

        return pl.pallas_call(
            body,
            out_shape=jax.ShapeDtypeStruct(right_side.shape, F32),
            in_specs=[pl.BlockSpec(memory_space=pl.ANY)] * 3,
            out_specs=pl.BlockSpec(memory_space=pl.ANY),
            scratch_shapes=list(shapes.values()),
            compiler_params=pltpu.CompilerParams(
                collective_id=0, has_side_effects=True, vmem_limit_bytes=40 * 1024 * 1024
            ),
        )(right_side, base_coef, cell_type)

    placed = P("ht", "az", None)
    return jax.shard_map(
        on_device, mesh=mesh, in_specs=(placed,) * 3, out_specs=placed, check_vma=False
    )
```

```python
import jax
import jax.numpy as jnp
from jax import lax
from jax.experimental import pallas as pl
from jax.experimental.pallas import tpu as pltpu
from jax.sharding import PartitionSpec as P

DEGREE = 4
COARSE_SWEEPS = 6

shift_value = 0.002
smooth_low = 0.3
coarse_low = 0.02
high_end = 2.0

F32 = jnp.float32
BF16 = jnp.bfloat16
MESH = pl.DeviceIdType.MESH

NEAR = [(1, 1), (1, -1), (1, 0), (-1, 1), (-1, -1), (-1, 0), (0, 1), (0, -1)]
REACH = 2


def chebyshev_steps(degree, low_end):
    middle = 0.5 * (high_end + low_end)
    spread = 0.5 * (high_end - low_end)
    sigma_ratio = middle / spread
    rho_now = 1.0 / sigma_ratio
    steps = []
    for _ in range(degree - 1):
        rho_next = 1.0 / (2.0 * sigma_ratio - rho_now)
        keep, add = rho_next * rho_now, 2.0 * rho_next / spread
        steps.append((1.0 + keep - add, keep, add))
        rho_now = rho_next
    return 1.0 / middle, steps


def exact_dot(values, weights):
    count = values.shape[0]
    high = values.astype(BF16)
    rest = values - high.astype(F32)
    mid = rest.astype(BF16)
    low = (rest - mid.astype(F32)).astype(BF16)
    pieces = jnp.concatenate([high, mid, low], axis=0)
    total = jnp.dot(pieces, weights, preferred_element_type=F32)
    return total[0:count] + total[count : 2 * count] + total[2 * count :]


def each_row(start, count, block, body):
    if block >= count:
        for i in range(count):
            body(start + i)
        return

    def step(i, carry):
        for j in range(block):
            body(start + i * block + j)
        return carry

    lax.fori_loop(0, count // block, step, 0)


def next_in(values, axis):
    return pltpu.roll(values, values.shape[axis] - 1, axis)


def last_in(values, axis):
    return pltpu.roll(values, 1, axis)


def iotas(shape):
    return lax.broadcasted_iota(jnp.int32, shape, 0), lax.broadcasted_iota(jnp.int32, shape, 1)


class Level:
    def __init__(self, s, level, own, spacing, low_end, degree):
        for name in ("k", "b", "x", "y", "up", "side", "out", "inv", "piv"):
            setattr(self, name, getattr(s, f"{name}{level}"))
        self.own_az, self.own_ht = own
        self.rows, self.sub, self.lanes = self.b.shape
        self.half = 0.5 * spacing
        self.first, self.steps = chebyshev_steps(degree, low_end)

    def clear(self):
        for field in (self.k, self.b):
            rest = field.at[:, self.own_ht :]
            rest[...] = jnp.zeros(rest.shape, F32)

    def set_up(self, block, below, above):
        sub, lane = iotas((self.sub, self.lanes))
        last_lane, first_lane = lane == self.lanes - 1, lane == 0
        top, bottom = sub == self.own_ht + 3, sub == self.own_ht + 4
        lost = ((sub >= self.own_ht) & (sub < self.own_ht + 4) & jnp.logical_not(above)) | (
            (sub >= self.own_ht + 4) & jnp.logical_not(below)
        )
        inside = jnp.where(lost, 0.0, 1.0).astype(F32)

        own, nearer = self.own_ht, iotas((8, self.lanes))[0] < 4

        def folded(i):
            halo = jnp.where(nearer, self.k[i, own : own + 8], self.k[i, own + 8 : own + 16])
            return jnp.concatenate([self.k[i, 0:own], halo], axis=0)

        def body(i):
            k = folded(i + 1)
            up = self.half * (k + folded(i + 2))
            down = self.half * (k + folded(i))
            fifth_up, fifth_down = self.k[i + 1, own + 4 : own + 5], self.k[i + 1, own + 11 : own + 12]
            side = self.half * (k + jnp.where(top, fifth_up, next_in(k, 0)))
            under = jnp.where(bottom, self.half * (k + fifth_down), last_in(side, 0))
            out = self.half * (k + jnp.where(last_lane, 0.0, next_in(k, 1)))
            back = jnp.where(first_lane, self.half * k, last_in(out, 1))
            piv = shift_value + (up + down + side + under + out + back)
            self.up[i], self.side[i], self.piv[i] = up, side, piv
            self.out[i] = jnp.where(last_lane, 0.0, out)
            self.inv[i] = inside / piv

        each_row(0, self.rows, block, body)

    def gathered(self, i):
        x, side, out = self.x[i], self.side[i], self.out[i]
        total = self.b[i] + self.up[i] * self.x[i + 1] + self.up[i - 1] * self.x[i - 1]
        total = total + (side * next_in(x, 0) + last_in(side * x, 0))
        return total + (out * next_in(x, 1) + last_in(out * x, 1)), x

    def smooth(self, blocks):
        def start(i):
            self.x[i] = self.b[i] * self.inv[i] * self.first

        each_row(0, self.rows, blocks[0], start)
        for number, (scale, keep, add) in enumerate(self.steps):

            def body(i):
                total, x = self.gathered(i)
                new = scale * x + add * (total * self.inv[i])
                self.y[i] = new - keep * self.y[i] if number else new

            each_row(number + 1, self.rows - 2 * (number + 1), blocks[number + 1], body)
            self.x, self.y = self.y, self.x

    def residual(self, i):
        total, x = self.gathered(i)
        return total - self.piv[i] * x


def span(step, layers, halo, own, here):
    if step == 0:
        return pl.ds(halo, own)
    if step == 1:
        return pl.ds(halo + own - layers if here else halo - layers, layers)
    return pl.ds(halo if here else halo + own, layers)


def span_up(step, layers, sub, own, here):
    if step == 0:
        return pl.ds(0, own)
    if step == 1:
        return pl.ds(own - layers if here else sub - layers, layers)
    return pl.ds(0 if here else own, layers)


def kernel(n_ht, n_az, rhs_hbm, coef_hbm, type_hbm, res, s):
    ht, az = lax.axis_index("ht"), lax.axis_index("az")
    has = {1: ht < n_ht - 1, -1: ht > 0}
    cols, rows, _ = rhs_hbm.shape
    mid_cols, mid_rows = cols // 2, rows // 2
    low_cols = mid_cols // 2
    fine = Level(s, 0, (cols, rows), 1.0, smooth_low, DEGREE)
    middle = Level(s, 1, (mid_cols, mid_rows), 0.25, smooth_low, DEGREE)

    def there(dh, run):
        if dh == 0:
            run()
        else:
            pl.when(has[dh])(run)

    loads = [
        pltpu.make_async_copy(coef_hbm, s.coef, s.load_sem.at[0]),
        pltpu.make_async_copy(type_hbm, s.kind, s.load_sem.at[1]),
        pltpu.make_async_copy(rhs_hbm, s.b0.at[pl.ds(4, cols), pl.ds(0, rows)], s.load_sem.at[2]),
    ]
    for load in loads:
        load.start()

    fine.clear()
    middle.clear()
    far = [
        (dh, da)
        for da in (2, -2, 1, -1, 0)
        for dh in (2, 1, 3, 0)[4 - n_ht :]
        if (dh, da) != (0, 0)
    ]

    def far_device(dh, da):
        return {"ht": lax.rem(ht + dh, n_ht), "az": lax.rem(az + (da + n_az), n_az)}

    barrier = pltpu.get_barrier_semaphore()
    met = [(dh, da) for dh, da in far if abs(da) < 2]
    for dh, da in met:
        pl.semaphore_signal(barrier, inc=1, device_id=far_device(dh, da), device_id_type=MESH)

    sent = []

    def grouped(copies, act):
        for dh in (1, -1, 0):
            group = [copy for step, copy in copies if step == dh]

            def run(group=group):
                for copy in group:
                    act(copy)

            there(dh, run)

    def exchange(slot, field, level, halo, layers, corner_layers):
        made = []
        for i, (dh, da) in enumerate(NEAR):
            deep = corner_layers if dh and da else layers

            def part(here):
                return field.at[
                    span(da, deep, halo, level.own_az, here),
                    span_up(dh, deep, field.shape[1], level.own_ht, here),
                ]

            copy = pltpu.make_async_remote_copy(
                src_ref=part(True),
                dst_ref=part(False),
                send_sem=s.send_sem.at[slot + i],
                recv_sem=s.recv_sem.at[slot + i],
                device_id={"ht": ht + dh, "az": lax.rem(az + (da + n_az), n_az)},
                device_id_type=MESH,
            )
            made.append((dh, copy))
        grouped(made, lambda copy: copy.start())
        sent.extend(made)
        return made

    def arrived(made):
        grouped([(-dh, copy) for dh, copy in made], lambda copy: copy.wait_recv())

    loads[0].wait()
    loads[1].wait()

    def conductivity(a):
        kind = s.kind[a]
        factor = jnp.where(kind == 0, 0.1, jnp.where(kind == 1, 0.4, 1.0)).astype(F32)
        s.k0[5 + a, 0:rows] = s.coef[a] * factor

    each_row(0, cols, 6, conductivity)
    loads[2].wait()
    pl.semaphore_wait(barrier, len(met))
    k_fine = exchange(0, s.k0, fine, 5, 5, 4)
    b_fine = exchange(8, s.b0, fine, 4, 4, 3)

    def as_weights(picked, value):
        return jnp.where(picked, value, 0.0).astype(BF16)

    i, j = iotas(s.down0.shape)
    s.down0[...] = as_weights(i // 2 == j, 0.125)
    i, j = iotas(s.down1.shape)
    s.down1[...] = as_weights(i // 2 == j % 64, 0.125)
    i, j = iotas(s.wide0.shape)
    s.wide0[...] = as_weights(i == j // 2, 1.0)
    i, j = iotas(s.wide1.shape)
    s.wide1[...] = as_weights(i == j // 2, 1.0)

    sub, lane = iotas((8, 128))
    front = lane < 64
    even = sub % 2 == 0

    def restrict0(pair):
        pairs = jnp.concatenate([pair(i) for i in range(mid_cols)], axis=0)
        s.halves[...] = exact_dot(pairs, s.down0[...])
        count = mid_cols * mid_rows
        means = s.halves[pl.ds(0, count, stride=2), :] + s.halves[pl.ds(1, count, stride=2), :]
        return means.reshape(mid_cols, mid_rows, -1)

    def restrict1(pair):
        sums = exact_dot(jnp.concatenate([pair(i) for i in range(low_cols)], axis=0), s.down1[...])
        packed = []
        for i in range(low_cols):
            mean = sums[8 * i : 8 * i + 8]
            mean = mean + next_in(mean, 0)
            mean = jnp.where(front, mean, pltpu.roll(mean, 4, 0))
            packed.append(jnp.where(sub == 1, next_in(mean, 0), mean))
        return packed

    def spread(kept, field, number):
        block = kept.at[:, pl.ds(0, 2)]

        def place(da):
            return field.at[pl.ds((REACH - da) * low_cols, low_cols), pl.ds(2 * ht, 2)]

        for dh, da in far:
            pltpu.make_async_remote_copy(
                src_ref=block,
                dst_ref=place(da),
                send_sem=s.far_send.at[number],
                recv_sem=s.far_recv.at[number],
                device_id=far_device(dh, da),
                device_id_type=MESH,
            ).start()
        pltpu.make_async_copy(block, place(0), s.far_recv.at[number]).start()

    def all_in(field, number):
        pltpu.make_async_copy(field, field, s.far_recv.at[number]).wait()

    kappa1 = restrict0(lambda i: s.k0[5 + 2 * i, 0:rows] + s.k0[6 + 2 * i, 0:rows])
    s.k1[5 : 5 + mid_cols, 0:mid_rows] = kappa1
    k_middle = exchange(16, s.k1, middle, 5, 5, 4)
    kappa2 = restrict1(lambda i: kappa1[2 * i] + kappa1[2 * i + 1])
    for i, block in enumerate(kappa2):
        s.kept_k[i] = block

    arrived(k_fine)
    fine.set_up(4, has[-1], has[1])
    arrived(b_fine)
    fine.smooth((10, 6, 4, 7))

    def pair_of_residual(i):
        pair = fine.residual(4 + 2 * i) + fine.residual(5 + 2 * i)
        s.pairs[i] = pair[0:rows]

    each_row(0, mid_cols, 3, pair_of_residual)
    s.b1[4 : 4 + mid_cols, 0:mid_rows] = restrict0(lambda i: s.pairs[i])
    b_middle = exchange(24, s.b1, middle, 4, 4, 3)
    spread(s.kept_k, s.k2, 0)

    arrived(k_middle)
    middle.set_up(7, has[-1], has[1])
    arrived(b_middle)
    middle.smooth((14, 12, 10, 8))
    r1 = [middle.residual(4 + i)[0:mid_rows] for i in range(mid_cols)]
    for i, block in enumerate(restrict1(lambda i: r1[2 * i] + r1[2 * i + 1])):
        s.kept_b[i] = block
    spread(s.kept_b, s.b2, 1)

    inner_last, inner_first = lane % 64 == 63, lane % 64 == 0
    top = (sub == 2 * n_ht - 1) & jnp.logical_not(front)
    bottom = (sub == 0) & front

    def up_and_down(x):
        ahead, behind = next_in(x, 0), last_in(x, 0)
        swapped = pltpu.roll(jnp.where(front, ahead, behind), 64, 1)
        return jnp.where(even, ahead, swapped), jnp.where(even, swapped, behind)

    all_in(s.k2, 0)
    half = 0.5 * 0.0625
    reach = low_cols * REACH
    for a in range(1, 2 * reach + low_cols - 1):
        k = s.k2[a]
        above, below = up_and_down(k)
        above = half * (k + jnp.where(top, 0.0, above))
        below = half * (k + jnp.where(bottom, 0.0, below))
        up = half * (k + s.k2[a + 1])
        down = half * (k + s.k2[a - 1])
        out = half * (k + jnp.where(inner_last, 0.0, next_in(k, 1)))
        back = jnp.where(inner_first, half * k, last_in(out, 1))
        s.inv2[a] = 1.0 / (shift_value + (up + down + above + below + out + back))
        s.up2[a] = up
        s.above2[a] = jnp.where(top, 0.0, above)
        s.below2[a] = jnp.where(bottom, 0.0, below)
        s.out2[a] = jnp.where(inner_last, 0.0, out)

    all_in(s.b2, 1)
    first, steps = chebyshev_steps(COARSE_SWEEPS, coarse_low)
    size = 2 * reach + low_cols
    x = [None] + [s.b2[a] * s.inv2[a] * first for a in range(1, size - 1)] + [None]
    before = [None] * size
    for number, (scale, keep, add) in enumerate(steps):
        new = [None] * size
        for a in range(number + 2, size - number - 2):
            above, below = up_and_down(x[a])
            total = s.b2[a] + s.up2[a] * x[a + 1] + s.up2[a - 1] * x[a - 1]
            total = total + (s.above2[a] * above + s.below2[a] * below)
            out = s.out2[a]
            total = total + (out * next_in(x[a], 1) + last_in(out * x[a], 1))
            new[a] = scale * x[a] + add * (total * s.inv2[a])
            if number:
                new[a] = new[a] - keep * before[a]
        x, before = new, x

    tiles = []
    for i in range(low_cols):
        mine = pltpu.roll(x[reach + i], lax.rem(2 * n_ht - 2 * ht, 2 * n_ht), 0)
        mine = jnp.where(sub // 2 % 2 == 0, mine[0:1], mine[1:2])
        tiles.append(jnp.where(sub < 4, mine, pltpu.roll(mine, 64, 1)))
    raised = exact_dot(jnp.concatenate(tiles, axis=0), s.wide1[...])
    parts = [
        middle.x[4 + i, 0:mid_rows] + raised[8 * (i // 2) : 8 * (i // 2) + 8] for i in range(mid_cols)
    ]
    parts = jnp.concatenate(parts, axis=0)
    count = mid_cols * mid_rows
    s.doubled[pl.ds(0, count, stride=2), :] = parts
    s.doubled[pl.ds(1, count, stride=2), :] = parts
    raised = exact_dot(s.doubled[...], s.wide0[...])
    for a in range(cols):
        res[a] = fine.x[4 + a, 0:rows] + raised[rows * (a // 2) : rows * (a // 2) + rows]

    grouped(sent, lambda copy: copy.wait_send())
    for number in range(2):
        pltpu.make_async_copy(s.tally, s.tally, s.far_send.at[number]).wait()


class Scratch:
    pass


def scratch_shapes(cols, rows, lanes, n_ht):
    mid_cols, mid_rows, mid_lanes = cols // 2, rows // 2, lanes // 2
    low_cols = mid_cols // 2
    others = (2 * REACH + 1) * n_ht - 1
    fields = {
        "coef": (cols, rows, lanes),
        "pairs": (mid_cols, rows, lanes),
        "halves": (mid_cols * rows, mid_lanes),
        "doubled": (mid_cols * rows, mid_lanes),
        "kept_k": (low_cols, 8, 128),
        "kept_b": (low_cols, 8, 128),
        "tally": (others * low_cols, 2, 128),
    }
    for level, (size, sub, width) in enumerate([(cols, rows + 8, lanes), (mid_cols, mid_rows + 8, mid_lanes)]):
        fields[f"k{level}"] = (size + 10, sub + 8, width)
        for name in ("b", "x", "y", "up", "side", "out", "inv", "piv"):
            fields[f"{name}{level}"] = (size + 8, sub, width)
    for name in ("k2", "b2", "up2", "above2", "below2", "out2", "inv2"):
        fields[name] = ((2 * REACH + 1) * low_cols, 2 * n_ht, 128)
    shapes = {name: pltpu.VMEM(shape, F32) for name, shape in fields.items()}
    shapes["kind"] = pltpu.VMEM((cols, rows, lanes), jnp.int32)
    shapes["down0"] = pltpu.VMEM((lanes, mid_lanes), BF16)
    shapes["down1"] = pltpu.VMEM((mid_lanes, 128), BF16)
    shapes["wide0"] = pltpu.VMEM((mid_lanes, lanes), BF16)
    shapes["wide1"] = pltpu.VMEM((128, mid_lanes), BF16)
    shapes["load_sem"] = pltpu.SemaphoreType.DMA((3,))
    shapes["send_sem"] = pltpu.SemaphoreType.DMA((32,))
    shapes["recv_sem"] = pltpu.SemaphoreType.DMA((32,))
    shapes["far_send"] = pltpu.SemaphoreType.DMA((2,))
    shapes["far_recv"] = pltpu.SemaphoreType.DMA((2,))
    return shapes


def solution(mesh):
    n_ht, n_az = mesh.shape["ht"], mesh.shape["az"]

    def on_device(right_side, base_coef, cell_type):
        blocks = [jnp.transpose(block, (1, 0, 2)) for block in (right_side, base_coef, cell_type)]
        shape = blocks[0].shape
        shapes = scratch_shapes(*shape, n_ht)

        def body(rhs, coef, kind, res, *refs):
            s = Scratch()
            for name, ref in zip(shapes, refs):
                setattr(s, name, ref)
            kernel(n_ht, n_az, rhs, coef, kind, res, s)

        result = pl.pallas_call(
            body,
            out_shape=pltpu.VMEM(shape, F32),
            in_specs=[pl.BlockSpec(memory_space=pltpu.HBM)] * 3,
            out_specs=pl.BlockSpec(memory_space=pltpu.VMEM),
            scratch_shapes=list(shapes.values()),
            compiler_params=pltpu.CompilerParams(
                collective_id=0, has_side_effects=True, vmem_limit_bytes=56 * 1024 * 1024
            ),
        )(*blocks)
        return jnp.transpose(result, (1, 0, 2))

    placed = P("ht", "az", None)
    return jax.shard_map(
        on_device, mesh=mesh, in_specs=(placed,) * 3, out_specs=placed, check_vma=False
    )
```

```python
import jax
import jax.numpy as jnp
from jax import lax
from jax.experimental import pallas as pl
from jax.experimental.pallas import tpu as pltpu
from jax.sharding import PartitionSpec as P

DEGREE = 4
COARSE_SWEEPS = 6

shift_value = 0.002
smooth_low = 0.3
coarse_low = 0.02
high_end = 2.0

F32 = jnp.float32
BF16 = jnp.bfloat16
MESH = pl.DeviceIdType.MESH

SIDES = [(0, 1), (0, -1)]
ENDS = [(1, 0), (-1, 0)]
CORNERS = [(1, 1), (1, -1), (-1, 1), (-1, -1)]
NEAR = SIDES + ENDS + CORNERS
REACH = 2


def chebyshev_steps(degree, low_end):
    middle = 0.5 * (high_end + low_end)
    spread = 0.5 * (high_end - low_end)
    sigma_ratio = middle / spread
    rho_now = 1.0 / sigma_ratio
    steps = []
    for _ in range(degree - 1):
        rho_next = 1.0 / (2.0 * sigma_ratio - rho_now)
        keep, add = rho_next * rho_now, 2.0 * rho_next / spread
        steps.append((1.0 + keep - add, keep, add))
        rho_now = rho_next
    return 1.0 / middle, steps


def exact_dot(values, weights):
    count = values.shape[0]
    high = values.astype(BF16)
    rest = values - high.astype(F32)
    mid = rest.astype(BF16)
    low = (rest - mid.astype(F32)).astype(BF16)
    pieces = jnp.concatenate([high, mid, low], axis=0)
    total = jnp.dot(pieces, weights, preferred_element_type=F32)
    return total[0:count] + total[count : 2 * count] + total[2 * count :]


def each_row(ranges, body):
    for first, count, block in ranges:
        if block >= count:
            for i in range(count):
                body(first + i)
            continue

        def step(i, carry, first=first, block=block):
            for j in range(block):
                body(first + i * block + j)
            return carry

        lax.fori_loop(0, count // block, step, 0)


def next_in(values, axis):
    return pltpu.roll(values, values.shape[axis] - 1, axis)


def last_in(values, axis):
    return pltpu.roll(values, 1, axis)


def iotas(shape):
    return lax.broadcasted_iota(jnp.int32, shape, 0), lax.broadcasted_iota(jnp.int32, shape, 1)


class Level:
    def __init__(self, s, level, own, spacing, low_end, degree):
        for name in ("k", "b", "x", "y", "up", "side", "out", "inv", "piv"):
            setattr(self, name, getattr(s, f"{name}{level}"))
        self.own_az, self.own_ht = own
        self.rows, self.sub, self.lanes = self.b.shape
        self.half = 0.5 * spacing
        self.first, self.steps = chebyshev_steps(degree, low_end)

    def clear(self):
        for field in (self.k, self.b):
            rest = field.at[:, self.own_ht :]
            rest[...] = jnp.zeros(rest.shape, F32)

    def set_up(self, ranges, below, above):
        sub, lane = iotas((self.sub, self.lanes))
        last_lane, first_lane = lane == self.lanes - 1, lane == 0
        top, bottom = sub == self.own_ht + 3, sub == self.own_ht + 4
        lost = ((sub >= self.own_ht) & (sub < self.own_ht + 4) & jnp.logical_not(above)) | (
            (sub >= self.own_ht + 4) & jnp.logical_not(below)
        )
        inside = jnp.where(lost, 0.0, 1.0).astype(F32)

        own, nearer = self.own_ht, iotas((8, self.lanes))[0] < 4

        def folded(i):
            halo = jnp.where(nearer, self.k[i, own : own + 8], self.k[i, own + 8 : own + 16])
            return jnp.concatenate([self.k[i, 0:own], halo], axis=0)

        def body(i):
            k = folded(i + 1)
            up = self.half * (k + folded(i + 2))
            down = self.half * (k + folded(i))
            fifth_up, fifth_down = self.k[i + 1, own + 4 : own + 5], self.k[i + 1, own + 11 : own + 12]
            side = self.half * (k + jnp.where(top, fifth_up, next_in(k, 0)))
            under = jnp.where(bottom, self.half * (k + fifth_down), last_in(side, 0))
            out = self.half * (k + jnp.where(last_lane, 0.0, next_in(k, 1)))
            back = jnp.where(first_lane, self.half * k, last_in(out, 1))
            piv = shift_value + (up + down + side + under + out + back)
            self.up[i], self.side[i], self.piv[i] = up, side, piv
            self.out[i] = jnp.where(last_lane, 0.0, out)
            self.inv[i] = inside / piv

        each_row(ranges, body)

    def gathered(self, field, i):
        x, side, out = field[i], self.side[i], self.out[i]
        total = self.b[i] + self.up[i] * field[i + 1] + self.up[i - 1] * field[i - 1]
        total = total + (side * next_in(x, 0) + last_in(side * x, 0))
        return total + (out * next_in(x, 1) + last_in(out * x, 1)), x

    def start(self, ranges):
        def body(i):
            self.x[i] = self.b[i] * self.inv[i] * self.first

        each_row(ranges, body)

    def sweep(self, number, ranges):
        scale, keep, add = self.steps[number]
        old, new = self.fields(number)

        def body(i):
            total, x = self.gathered(old, i)
            value = scale * x + add * (total * self.inv[i])
            new[i] = value - keep * new[i] if number else value

        each_row(ranges, body)

    def fields(self, number):
        return (self.y, self.x) if number % 2 else (self.x, self.y)

    def result(self):
        return self.fields(len(self.steps))[0]

    def residual(self, i):
        total, x = self.gathered(self.result(), i)
        return total - self.piv[i] * x


def span(step, layers, halo, own, here):
    if step == 0:
        return pl.ds(halo, own)
    if step == 1:
        return pl.ds(halo + own - layers if here else halo - layers, layers)
    return pl.ds(halo if here else halo + own, layers)


def span_up(step, layers, sub, own, here):
    if step == 0:
        return pl.ds(0, own)
    if step == 1:
        return pl.ds(own - layers if here else sub - layers, layers)
    return pl.ds(0 if here else own, layers)


def kernel(n_ht, n_az, rhs_hbm, coef_hbm, type_hbm, res, s):
    ht, az = lax.axis_index("ht"), lax.axis_index("az")
    has = {1: ht < n_ht - 1, -1: ht > 0}
    cols, rows, _ = rhs_hbm.shape
    mid_cols, mid_rows = cols // 2, rows // 2
    low_cols = mid_cols // 2
    fine = Level(s, 0, (cols, rows), 1.0, smooth_low, DEGREE)
    middle = Level(s, 1, (mid_cols, mid_rows), 0.25, smooth_low, DEGREE)

    def there(dh, run):
        if dh == 0:
            run()
        else:
            pl.when(has[dh])(run)

    @pl.when(jnp.logical_not(has[1] & has[-1]))
    def _():
        fine.clear()
        middle.clear()

    s.k2[...] = jnp.zeros_like(s.k2)
    s.b2[...] = jnp.zeros_like(s.b2)

    def device(dh, da):
        return {"ht": ht + dh, "az": lax.rem(az + (da + n_az), n_az)}

    def grouped(copies, act):
        for dh in (1, -1, 0):
            group = [copy for step, copy in copies if step == dh]

            def run(group=group):
                for copy in group:
                    act(copy)

            there(dh, run)

    barrier = pltpu.get_barrier_semaphore()
    grouped(
        [(dh, (dh, da)) for dh, da in CORNERS + ENDS + SIDES],
        lambda step: pl.semaphore_signal(barrier, inc=1, device_id=device(*step), device_id_type=MESH),
    )
    loads = [
        pltpu.make_async_copy(coef_hbm, s.coef, s.load_sem.at[0]),
        pltpu.make_async_copy(type_hbm, s.kind, s.load_sem.at[1]),
        pltpu.make_async_copy(rhs_hbm, s.b0.at[pl.ds(4, cols), pl.ds(0, rows)], s.load_sem.at[2]),
    ]
    for load in loads:
        load.start()

    sent = []

    def exchange(slot, directions, field, level, halo, layers):
        made = []
        for dh, da in directions:

            def part(here):
                return field.at[
                    span(da, layers, halo, level.own_az, here),
                    span_up(dh, layers, field.shape[1], level.own_ht, here),
                ]

            number = slot + NEAR.index((dh, da))
            copy = pltpu.make_async_remote_copy(
                src_ref=part(True),
                dst_ref=part(False),
                send_sem=s.send_sem.at[number],
                recv_sem=s.recv_sem.at[number],
                device_id=device(dh, da),
                device_id_type=MESH,
            )
            made.append((dh, copy))
        grouped(made, lambda copy: copy.start())
        sent.extend(made)
        return made

    def arrived(made):
        grouped([(-dh, copy) for dh, copy in made], lambda copy: copy.wait_recv())

    loads[0].wait()
    loads[1].wait()

    def conductivity(a):
        kind = s.kind[a]
        factor = jnp.where(kind == 0, 0.1, jnp.where(kind == 1, 0.4, 1.0)).astype(F32)
        s.k0[5 + a, 0:rows] = s.coef[a] * factor

    each_row([(0, cols, 6)], conductivity)
    ends = jnp.where(has[1], 1, 0) + jnp.where(has[-1], 1, 0)
    pl.semaphore_wait(barrier, 2 + 3 * ends)
    k_sides = exchange(0, CORNERS, s.k0, fine, 5, 4)
    k_ends = exchange(0, ENDS, s.k0, fine, 5, 5)
    k_sides += exchange(0, SIDES, s.k0, fine, 5, 5)
    loads[2].wait()
    b_sides = exchange(8, CORNERS, s.b0, fine, 4, 3)
    b_ends = exchange(8, ENDS, s.b0, fine, 4, 4)
    b_sides += exchange(8, SIDES, s.b0, fine, 4, 4)

    def as_weights(picked, value):
        return jnp.where(picked, value, 0.0).astype(BF16)

    i, j = iotas(s.down0.shape)
    s.down0[...] = as_weights(i // 2 == j, 0.125)
    i, j = iotas(s.down1.shape)
    s.down1[...] = as_weights(i // 2 == j % 64, 0.125)
    i, j = iotas(s.wide0.shape)
    s.wide0[...] = as_weights(i == j // 2, 1.0)
    i, j = iotas(s.wide1.shape)
    s.wide1[...] = as_weights(i == j // 2, 1.0)

    sub, lane = iotas((8, 128))
    front = lane < 64
    even = sub % 2 == 0

    def restrict0(pair):
        pairs = jnp.concatenate([pair(i) for i in range(mid_cols)], axis=0)
        s.halves[...] = exact_dot(pairs, s.down0[...])
        count = mid_cols * mid_rows
        means = s.halves[pl.ds(0, count, stride=2), :] + s.halves[pl.ds(1, count, stride=2), :]
        return means.reshape(mid_cols, mid_rows, -1)

    def restrict1(pair):
        sums = exact_dot(jnp.concatenate([pair(i) for i in range(low_cols)], axis=0), s.down1[...])
        packed = []
        for i in range(low_cols):
            mean = sums[8 * i : 8 * i + 8]
            mean = mean + next_in(mean, 0)
            mean = jnp.where(front, mean, pltpu.roll(mean, 4, 0))
            packed.append(jnp.where(sub == 1, next_in(mean, 0), mean))
        return packed

    def spread(kept, field, first, groups):
        block = kept.at[:, pl.ds(0, 2)]

        def there_far(dh, run):
            if abs(dh) < 2:
                there(dh, run)
            else:
                pl.when((ht + dh >= 0) & (ht + dh < n_ht))(run)

        def place(da):
            return field.at[pl.ds((REACH - da) * low_cols, low_cols), pl.ds(2 * ht, 2)]

        for number, (dh, reached) in enumerate(groups, first):

            def go(dh=dh, reached=reached, number=number):
                for da in reached:
                    pltpu.make_async_remote_copy(
                        src_ref=block,
                        dst_ref=place(da),
                        send_sem=s.far_send.at[number],
                        recv_sem=s.far_recv.at[number],
                        device_id=device(dh, da),
                        device_id_type=MESH,
                    ).start()

            there_far(dh, go)
        own = pltpu.make_async_copy(block, place(0), s.own_sem.at[first // len(groups)])
        own.start()

        def finish(towards, sems):
            for number, (dh, reached) in enumerate(groups, first):
                some = s.tally.at[pl.ds(0, len(reached) * low_cols)]

                def wait(number=number, some=some):
                    pltpu.make_async_copy(some, some, sems.at[number]).wait()

                there_far(towards * dh, wait)
            if towards < 0:
                own.wait()

        return finish

    kappa1 = restrict0(lambda i: s.k0[5 + 2 * i, 0:rows] + s.k0[6 + 2 * i, 0:rows])
    s.k1[5 : 5 + mid_cols, 0:mid_rows] = kappa1
    k_middle = exchange(16, CORNERS, s.k1, middle, 5, 4)
    k_middle += exchange(16, ENDS + SIDES, s.k1, middle, 5, 5)
    kappa2 = restrict1(lambda i: kappa1[2 * i] + kappa1[2 * i + 1])
    for i, block in enumerate(kappa2):
        s.kept_k[i] = block

    last = fine.rows
    arrived(k_ends)
    fine.set_up([(5, cols - 2, 5)], has[-1], has[1])
    arrived(k_sides)
    fine.set_up([(0, 5, 5), (last - 5, 5, 5)], has[-1], has[1])
    arrived(b_ends)
    fine.start([(4, cols, 6)])
    for number, block in enumerate((5, 4, 6)):
        fine.sweep(number, [(5 + number, cols - 2 - 2 * number, block)])
    arrived(b_sides)
    fine.start([(0, 4, 4), (last - 4, 4, 4)])
    for number in range(len(fine.steps)):
        fine.sweep(number, [(1 + number, 4, 4), (last - 5 - number, 4, 4)])

    def pair_of_residual(i):
        pair = fine.residual(4 + 2 * i) + fine.residual(5 + 2 * i)
        s.pairs[i] = pair[0:rows]

    each_row([(0, mid_cols, 3)], pair_of_residual)
    s.b1[4 : 4 + mid_cols, 0:mid_rows] = restrict0(lambda i: s.pairs[i])
    b_middle = exchange(24, CORNERS, s.b1, middle, 4, 3)
    b_middle += exchange(24, ENDS + SIDES, s.b1, middle, 4, 4)
    around = [2, -2, 1, -1]
    k_coarse = spread(s.kept_k, s.k2, 0, [(1, around + [0]), (-1, around + [0]), (2, [1, -1, 0]), (-2, [1, -1, 0]), (0, around)])

    arrived(k_middle)
    middle.set_up([(0, middle.rows, 7)], has[-1], has[1])
    arrived(b_middle)
    middle.start([(0, middle.rows, middle.rows)])
    for number in range(len(middle.steps)):
        count = middle.rows - 2 - 2 * number
        middle.sweep(number, [(1 + number, count, count)])
    r1 = [middle.residual(4 + i)[0:mid_rows] for i in range(mid_cols)]
    for i, block in enumerate(restrict1(lambda i: r1[2 * i] + r1[2 * i + 1])):
        s.kept_b[i] = block
    b_coarse = spread(s.kept_b, s.b2, 5, [(1, around + [0]), (-1, around + [0]), (2, [0]), (-2, [0]), (0, around)])

    inner_last, inner_first = lane % 64 == 63, lane % 64 == 0
    top = (sub == 2 * n_ht - 1) & jnp.logical_not(front)
    bottom = (sub == 0) & front

    def up_and_down(x):
        ahead, behind = next_in(x, 0), last_in(x, 0)
        swapped = pltpu.roll(jnp.where(front, ahead, behind), 64, 1)
        return jnp.where(even, ahead, swapped), jnp.where(even, swapped, behind)

    k_coarse(-1, s.far_recv)
    half = 0.5 * 0.0625
    reach = low_cols * REACH
    for a in range(1, 2 * reach + low_cols - 1):
        k = s.k2[a]
        above, below = up_and_down(k)
        above = half * (k + jnp.where(top, 0.0, above))
        below = half * (k + jnp.where(bottom, 0.0, below))
        up = half * (k + s.k2[a + 1])
        down = half * (k + s.k2[a - 1])
        out = half * (k + jnp.where(inner_last, 0.0, next_in(k, 1)))
        back = jnp.where(inner_first, half * k, last_in(out, 1))
        s.inv2[a] = 1.0 / (shift_value + (up + down + above + below + out + back))
        s.up2[a] = up
        s.above2[a] = jnp.where(top, 0.0, above)
        s.below2[a] = jnp.where(bottom, 0.0, below)
        s.out2[a] = jnp.where(inner_last, 0.0, out)

    b_coarse(-1, s.far_recv)
    first, steps = chebyshev_steps(COARSE_SWEEPS, coarse_low)
    size = 2 * reach + low_cols
    x = [None] + [s.b2[a] * s.inv2[a] * first for a in range(1, size - 1)] + [None]
    before = [None] * size
    for number, (scale, keep, add) in enumerate(steps):
        new = [None] * size
        for a in range(number + 2, size - number - 2):
            above, below = up_and_down(x[a])
            total = s.b2[a] + s.up2[a] * x[a + 1] + s.up2[a - 1] * x[a - 1]
            total = total + (s.above2[a] * above + s.below2[a] * below)
            out = s.out2[a]
            total = total + (out * next_in(x[a], 1) + last_in(out * x[a], 1))
            new[a] = scale * x[a] + add * (total * s.inv2[a])
            if number:
                new[a] = new[a] - keep * before[a]
        x, before = new, x

    tiles = []
    for i in range(low_cols):
        mine = pltpu.roll(x[reach + i], lax.rem(2 * n_ht - 2 * ht, 2 * n_ht), 0)
        mine = jnp.where(sub // 2 % 2 == 0, mine[0:1], mine[1:2])
        tiles.append(jnp.where(sub < 4, mine, pltpu.roll(mine, 64, 1)))
    raised = exact_dot(jnp.concatenate(tiles, axis=0), s.wide1[...])
    parts = [
        middle.result()[4 + i, 0:mid_rows] + raised[8 * (i // 2) : 8 * (i // 2) + 8] for i in range(mid_cols)
    ]
    parts = jnp.concatenate(parts, axis=0)
    count = mid_cols * mid_rows
    s.doubled[pl.ds(0, count, stride=2), :] = parts
    s.doubled[pl.ds(1, count, stride=2), :] = parts
    raised = exact_dot(s.doubled[...], s.wide0[...])
    for a in range(cols):
        res[a] = fine.result()[4 + a, 0:rows] + raised[rows * (a // 2) : rows * (a // 2) + rows]

    grouped(sent, lambda copy: copy.wait_send())
    k_coarse(1, s.far_send)
    b_coarse(1, s.far_send)


class Scratch:
    pass


def scratch_shapes(cols, rows, lanes, n_ht):
    mid_cols, mid_rows, mid_lanes = cols // 2, rows // 2, lanes // 2
    low_cols = mid_cols // 2
    fields = {
        "coef": (cols, rows, lanes),
        "pairs": (mid_cols, rows, lanes),
        "halves": (mid_cols * rows, mid_lanes),
        "doubled": (mid_cols * rows, mid_lanes),
        "kept_k": (low_cols, 8, 128),
        "kept_b": (low_cols, 8, 128),
        "tally": ((2 * REACH + 1) * low_cols, 2, 128),
    }
    for level, (size, sub, width) in enumerate([(cols, rows + 8, lanes), (mid_cols, mid_rows + 8, mid_lanes)]):
        fields[f"k{level}"] = (size + 10, sub + 8, width)
        for name in ("b", "x", "y", "up", "side", "out", "inv", "piv"):
            fields[f"{name}{level}"] = (size + 8, sub, width)
    for name in ("k2", "b2", "up2", "above2", "below2", "out2", "inv2"):
        fields[name] = ((2 * REACH + 1) * low_cols, 2 * n_ht, 128)
    shapes = {name: pltpu.VMEM(shape, F32) for name, shape in fields.items()}
    shapes["kind"] = pltpu.VMEM((cols, rows, lanes), jnp.int32)
    shapes["down0"] = pltpu.VMEM((lanes, mid_lanes), BF16)
    shapes["down1"] = pltpu.VMEM((mid_lanes, 128), BF16)
    shapes["wide0"] = pltpu.VMEM((mid_lanes, lanes), BF16)
    shapes["wide1"] = pltpu.VMEM((128, mid_lanes), BF16)
    shapes["load_sem"] = pltpu.SemaphoreType.DMA((3,))
    shapes["send_sem"] = pltpu.SemaphoreType.DMA((32,))
    shapes["recv_sem"] = pltpu.SemaphoreType.DMA((32,))
    shapes["own_sem"] = pltpu.SemaphoreType.DMA((2,))
    shapes["far_send"] = pltpu.SemaphoreType.DMA((10,))
    shapes["far_recv"] = pltpu.SemaphoreType.DMA((10,))
    return shapes


def solution(mesh):
    n_ht, n_az = mesh.shape["ht"], mesh.shape["az"]

    def on_device(right_side, base_coef, cell_type):
        blocks = [jnp.transpose(block, (1, 0, 2)) for block in (right_side, base_coef, cell_type)]
        shape = blocks[0].shape
        shapes = scratch_shapes(*shape, n_ht)

        def body(rhs, coef, kind, res, *refs):
            s = Scratch()
            for name, ref in zip(shapes, refs):
                setattr(s, name, ref)
            kernel(n_ht, n_az, rhs, coef, kind, res, s)

        result = pl.pallas_call(
            body,
            out_shape=pltpu.VMEM(shape, F32),
            in_specs=[pl.BlockSpec(memory_space=pltpu.HBM)] * 3,
            out_specs=pl.BlockSpec(memory_space=pltpu.VMEM),
            scratch_shapes=list(shapes.values()),
            compiler_params=pltpu.CompilerParams(
                collective_id=0, has_side_effects=True, vmem_limit_bytes=56 * 1024 * 1024
            ),
        )(*blocks)
        return jnp.transpose(result, (1, 0, 2))

    placed = P("ht", "az", None)
    return jax.shard_map(
        on_device, mesh=mesh, in_specs=(placed,) * 3, out_specs=placed, check_vma=False
    )
```

```python
import jax
import jax.numpy as jnp
from jax import lax
from jax.experimental import pallas as pl
from jax.experimental.pallas import tpu as pltpu
from jax.sharding import PartitionSpec as P

DEGREE = 4
COARSE_SWEEPS = 6

shift_value = 0.002
smooth_low = 0.3
coarse_low = 0.02
high_end = 2.0

F32 = jnp.float32
BF16 = jnp.bfloat16
MESH = pl.DeviceIdType.MESH

SIDES = [(0, 1), (0, -1)]
ENDS = [(1, 0), (-1, 0)]
CORNERS = [(1, 1), (1, -1), (-1, 1), (-1, -1)]
NEAR = SIDES + ENDS + CORNERS
REACH = 2


def chebyshev_steps(degree, low_end):
    middle = 0.5 * (high_end + low_end)
    spread = 0.5 * (high_end - low_end)
    sigma_ratio = middle / spread
    rho_now = 1.0 / sigma_ratio
    steps = []
    for _ in range(degree - 1):
        rho_next = 1.0 / (2.0 * sigma_ratio - rho_now)
        keep, add = rho_next * rho_now, 2.0 * rho_next / spread
        steps.append((1.0 + keep - add, keep, add))
        rho_now = rho_next
    return 1.0 / middle, steps


def exact_dot(values, weights):
    count = values.shape[0]
    high = values.astype(BF16)
    rest = values - high.astype(F32)
    mid = rest.astype(BF16)
    low = (rest - mid.astype(F32)).astype(BF16)
    pieces = jnp.concatenate([high, mid, low], axis=0)
    total = jnp.dot(pieces, weights, preferred_element_type=F32)
    return total[0:count] + total[count : 2 * count] + total[2 * count :]


def each_row(ranges, body):
    for first, count, block in ranges:
        if block >= count:
            for i in range(count):
                body(first + i)
            continue

        def step(i, carry, first=first, block=block):
            for j in range(block):
                body(first + i * block + j)
            return carry

        lax.fori_loop(0, count // block, step, 0)


def next_in(values, axis):
    return pltpu.roll(values, values.shape[axis] - 1, axis)


def last_in(values, axis):
    return pltpu.roll(values, 1, axis)


def iotas(shape):
    return lax.broadcasted_iota(jnp.int32, shape, 0), lax.broadcasted_iota(jnp.int32, shape, 1)


class Level:
    def __init__(self, s, level, own, spacing, low_end, degree):
        for name in ("k", "b", "x", "y", "up", "side", "out", "inv", "piv"):
            setattr(self, name, getattr(s, f"{name}{level}"))
        self.own_az, self.own_ht = own
        self.rows, self.sub, self.lanes = self.b.shape
        self.half = 0.5 * spacing
        self.first, self.steps = chebyshev_steps(degree, low_end)

    def clear(self):
        for field in (self.k, self.b):
            rest = field.at[:, self.own_ht :]
            rest[...] = jnp.zeros(rest.shape, F32)

    def set_up(self, ranges, below, above):
        sub, lane = iotas((self.sub, self.lanes))
        last_lane, first_lane = lane == self.lanes - 1, lane == 0
        top, bottom = sub == self.own_ht + 3, sub == self.own_ht + 4
        lost = ((sub >= self.own_ht) & (sub < self.own_ht + 4) & jnp.logical_not(above)) | (
            (sub >= self.own_ht + 4) & jnp.logical_not(below)
        )
        inside = jnp.where(lost, 0.0, 1.0).astype(F32)

        own, nearer = self.own_ht, iotas((8, self.lanes))[0] < 4

        def folded(i):
            halo = jnp.where(nearer, self.k[i, own : own + 8], self.k[i, own + 8 : own + 16])
            return jnp.concatenate([self.k[i, 0:own], halo], axis=0)

        def body(i):
            k = folded(i + 1)
            up = self.half * (k + folded(i + 2))
            down = self.half * (k + folded(i))
            fifth_up, fifth_down = self.k[i + 1, own + 4 : own + 5], self.k[i + 1, own + 11 : own + 12]
            side = self.half * (k + jnp.where(top, fifth_up, next_in(k, 0)))
            under = jnp.where(bottom, self.half * (k + fifth_down), last_in(side, 0))
            out = self.half * (k + jnp.where(last_lane, 0.0, next_in(k, 1)))
            back = jnp.where(first_lane, self.half * k, last_in(out, 1))
            piv = shift_value + (up + down + side + under + out + back)
            self.up[i], self.side[i], self.piv[i] = up, side, piv
            self.out[i] = jnp.where(last_lane, 0.0, out)
            self.inv[i] = inside / piv

        each_row(ranges, body)

    def gathered(self, field, i):
        x, side, out = field[i], self.side[i], self.out[i]
        total = self.b[i] + self.up[i] * field[i + 1] + self.up[i - 1] * field[i - 1]
        total = total + (side * next_in(x, 0) + last_in(side * x, 0))
        return total + (out * next_in(x, 1) + last_in(out * x, 1)), x

    def start(self, ranges):
        def body(i):
            self.x[i] = self.b[i] * self.inv[i] * self.first

        each_row(ranges, body)

    def sweep(self, number, ranges):
        scale, keep, add = self.steps[number]
        old, new = self.fields(number)

        def body(i):
            total, x = self.gathered(old, i)
            value = scale * x + add * (total * self.inv[i])
            new[i] = value - keep * new[i] if number else value

        each_row(ranges, body)

    def fields(self, number):
        return (self.y, self.x) if number % 2 else (self.x, self.y)

    def result(self):
        return self.fields(len(self.steps))[0]

    def residual(self, i):
        total, x = self.gathered(self.result(), i)
        return total - self.piv[i] * x


def span(step, layers, halo, own, here):
    if step == 0:
        return pl.ds(halo, own)
    if step == 1:
        return pl.ds(halo + own - layers if here else halo - layers, layers)
    return pl.ds(halo if here else halo + own, layers)


def span_up(step, layers, sub, own, here):
    if step == 0:
        return pl.ds(0, own)
    if step == 1:
        return pl.ds(own - layers if here else sub - layers, layers)
    return pl.ds(0 if here else own, layers)


def kernel(n_ht, n_az, rhs_hbm, coef_hbm, type_hbm, res, s):
    ht, az = lax.axis_index("ht"), lax.axis_index("az")
    has = {1: ht < n_ht - 1, -1: ht > 0}
    cols, rows, _ = rhs_hbm.shape
    mid_cols, mid_rows = cols // 2, rows // 2
    low_cols = mid_cols // 2
    fine = Level(s, 0, (cols, rows), 1.0, smooth_low, DEGREE)
    middle = Level(s, 1, (mid_cols, mid_rows), 0.25, smooth_low, DEGREE)

    def there(dh, run):
        if dh == 0:
            run()
        else:
            pl.when(has[dh])(run)

    @pl.when(jnp.logical_not(has[1] & has[-1]))
    def _():
        fine.clear()
        middle.clear()

    s.k2[...] = jnp.zeros_like(s.k2)
    s.b2[...] = jnp.zeros_like(s.b2)

    def device(dh, da):
        return {"ht": ht + dh, "az": lax.rem(az + (da + n_az), n_az)}

    def grouped(copies, act):
        for dh in (1, -1, 0):
            group = [copy for step, copy in copies if step == dh]

            def run(group=group):
                for copy in group:
                    act(copy)

            there(dh, run)

    barrier = pltpu.get_barrier_semaphore()
    grouped(
        [(dh, (dh, da)) for dh, da in ENDS + SIDES],
        lambda step: pl.semaphore_signal(barrier, inc=1, device_id=device(*step), device_id_type=MESH),
    )
    loads = [
        pltpu.make_async_copy(coef_hbm, s.coef, s.load_sem.at[0]),
        pltpu.make_async_copy(type_hbm, s.kind, s.load_sem.at[1]),
        pltpu.make_async_copy(rhs_hbm, s.b0.at[pl.ds(4, cols), pl.ds(0, rows)], s.load_sem.at[2]),
    ]
    for load in loads:
        load.start()

    sent = []

    def exchange(slot, directions, field, level, halo, layers):
        made = []
        for dh, da in directions:

            def part(here):
                return field.at[
                    span(da, layers, halo, level.own_az, here),
                    span_up(dh, layers, field.shape[1], level.own_ht, here),
                ]

            number = slot + NEAR.index((dh, da))
            copy = pltpu.make_async_remote_copy(
                src_ref=part(True),
                dst_ref=part(False),
                send_sem=s.send_sem.at[number],
                recv_sem=s.recv_sem.at[number],
                device_id=device(dh, da),
                device_id_type=MESH,
            )
            made.append((dh, copy))
        grouped(made, lambda copy: copy.start())
        sent.extend(made)
        return made

    def arrived(made):
        grouped([(-dh, copy) for dh, copy in made], lambda copy: copy.wait_recv())

    loads[0].wait()
    loads[1].wait()

    def conductivity(a):
        kind = s.kind[a]
        factor = jnp.where(kind == 0, 0.1, jnp.where(kind == 1, 0.4, 1.0)).astype(F32)
        s.k0[5 + a, 0:rows] = s.coef[a] * factor

    each_row([(0, cols, 6)], conductivity)
    ends = jnp.where(has[1], 1, 0) + jnp.where(has[-1], 1, 0)
    pl.semaphore_wait(barrier, 2 + ends)
    grouped(
        [(dh, (dh, da)) for dh, da in ENDS],
        lambda step: pl.semaphore_signal(s.ready, inc=1, device_id=device(*step), device_id_type=MESH),
    )
    k_sides = exchange(0, SIDES, s.k0, fine, 5, 5)
    k_ends = exchange(0, ENDS, s.k0, fine, 5, 5)
    loads[2].wait()
    b_ends = exchange(8, ENDS, s.b0, fine, 4, 4)
    pl.semaphore_wait(s.ready, ends)
    k_sides += exchange(0, CORNERS, s.k0, fine, 5, 4)
    b_sides = exchange(8, CORNERS, s.b0, fine, 4, 3)
    b_sides += exchange(8, SIDES, s.b0, fine, 4, 4)

    def as_weights(picked, value):
        return jnp.where(picked, value, 0.0).astype(BF16)

    i, j = iotas(s.down0.shape)
    s.down0[...] = as_weights(i // 2 == j, 0.125)
    i, j = iotas(s.down1.shape)
    s.down1[...] = as_weights(i // 2 == j % 64, 0.125)
    i, j = iotas(s.wide0.shape)
    s.wide0[...] = as_weights(i == j // 2, 1.0)
    i, j = iotas(s.wide1.shape)
    s.wide1[...] = as_weights(i == j // 4, 1.0)

    sub, lane = iotas((8, 128))
    front = lane < 64
    even = sub % 2 == 0

    def restrict0(pair):
        pairs = jnp.concatenate([pair(i) for i in range(mid_cols)], axis=0)
        s.halves[...] = exact_dot(pairs, s.down0[...])
        count = mid_cols * mid_rows
        means = s.halves[pl.ds(0, count, stride=2), :] + s.halves[pl.ds(1, count, stride=2), :]
        return means.reshape(mid_cols, mid_rows, -1)

    def restrict1(pair):
        sums = exact_dot(jnp.concatenate([pair(i) for i in range(low_cols)], axis=0), s.down1[...])
        packed = []
        for i in range(low_cols):
            mean = sums[8 * i : 8 * i + 8]
            mean = mean + next_in(mean, 0)
            mean = jnp.where(front, mean, pltpu.roll(mean, 4, 0))
            packed.append(jnp.where(sub == 1, next_in(mean, 0), mean))
        return packed

    def spread(kept, field, first, groups):
        block = kept.at[:, pl.ds(0, 2)]

        def there_far(dh, run):
            if abs(dh) < 2:
                there(dh, run)
            else:
                pl.when((ht + dh >= 0) & (ht + dh < n_ht))(run)

        def place(da):
            return field.at[pl.ds((REACH - da) * low_cols, low_cols), pl.ds(2 * ht, 2)]

        for number, (dh, reached) in enumerate(groups, first):

            def go(dh=dh, reached=reached, number=number):
                for da in reached:
                    pltpu.make_async_remote_copy(
                        src_ref=block,
                        dst_ref=place(da),
                        send_sem=s.far_send.at[number],
                        recv_sem=s.far_recv.at[number],
                        device_id=device(dh, da),
                        device_id_type=MESH,
                    ).start()

            there_far(dh, go)
        own = pltpu.make_async_copy(block, place(0), s.own_sem.at[first // len(groups)])
        own.start()

        def finish(towards, sems):
            for number, (dh, reached) in enumerate(groups, first):
                some = s.tally.at[pl.ds(0, len(reached) * low_cols)]

                def wait(number=number, some=some):
                    pltpu.make_async_copy(some, some, sems.at[number]).wait()

                there_far(towards * dh, wait)
            if towards < 0:
                own.wait()

        return finish

    kappa1 = restrict0(lambda i: s.k0[5 + 2 * i, 0:rows] + s.k0[6 + 2 * i, 0:rows])
    s.k1[5 : 5 + mid_cols, 0:mid_rows] = kappa1
    k_middle = exchange(16, CORNERS, s.k1, middle, 5, 4)
    k_middle += exchange(16, ENDS + SIDES, s.k1, middle, 5, 5)
    kappa2 = restrict1(lambda i: kappa1[2 * i] + kappa1[2 * i + 1])
    for i, block in enumerate(kappa2):
        s.kept_k[i] = block

    last = fine.rows
    arrived(k_ends)
    fine.set_up([(5, cols - 2, 5)], has[-1], has[1])
    arrived(k_sides)
    fine.set_up([(0, 5, 5), (last - 5, 5, 5)], has[-1], has[1])
    arrived(b_ends)
    fine.start([(4, cols, 6)])
    for number, block in enumerate((5, 4, 6)):
        fine.sweep(number, [(5 + number, cols - 2 - 2 * number, block)])
    arrived(b_sides)
    fine.start([(0, 4, 4), (last - 4, 4, 4)])
    for number in range(len(fine.steps)):
        fine.sweep(number, [(1 + number, 4, 4), (last - 5 - number, 4, 4)])

    r0 = [fine.residual(4 + i)[0:rows] for i in range(cols)]
    s.b1[4 : 4 + mid_cols, 0:mid_rows] = restrict0(lambda i: r0[2 * i] + r0[2 * i + 1])
    b_middle = exchange(24, CORNERS, s.b1, middle, 4, 3)
    b_near = exchange(24, ENDS, s.b1, middle, 4, 4)
    b_middle += exchange(24, SIDES, s.b1, middle, 4, 4)
    around = [2, -2, 1, -1]
    k_coarse = spread(s.kept_k, s.k2, 0, [(1, around + [0]), (-1, around + [0]), (2, [1, -1, 0]), (-2, [1, -1, 0]), (0, around)])

    arrived(k_middle)
    middle.set_up([(0, middle.rows, 7)], has[-1], has[1])
    last = middle.rows
    arrived(b_near)
    middle.start([(4, mid_cols, mid_cols)])
    for number in range(2):
        middle.sweep(number, [(5 + number, mid_cols - 2 - 2 * number, mid_cols)])
    arrived(b_middle)
    middle.start([(0, 4, 4), (last - 4, 4, 4)])
    for number in range(2):
        middle.sweep(number, [(1 + number, 4, 4), (last - 5 - number, 4, 4)])
    middle.sweep(2, [(3, last - 6, last)])
    r1 = [middle.residual(4 + i)[0:mid_rows] for i in range(mid_cols)]
    for i, block in enumerate(restrict1(lambda i: r1[2 * i] + r1[2 * i + 1])):
        s.kept_b[i] = block
    b_coarse = spread(s.kept_b, s.b2, 5, [(1, around + [0]), (-1, around + [0]), (2, [0]), (-2, [0]), (0, around)])

    parts = middle.result()[4 : 4 + mid_cols, 0:mid_rows].reshape(mid_cols * mid_rows, -1)
    count = mid_cols * mid_rows
    s.doubled[pl.ds(0, count, stride=2), :] = parts
    s.doubled[pl.ds(1, count, stride=2), :] = parts
    raised = exact_dot(s.doubled[...], s.wide0[...])
    for a in range(cols):
        res[a] = fine.result()[4 + a, 0:rows] + raised[rows * (a // 2) : rows * (a // 2) + rows]

    inner_last, inner_first = lane % 64 == 63, lane % 64 == 0
    top = (sub == 2 * n_ht - 1) & jnp.logical_not(front)
    bottom = (sub == 0) & front

    def up_and_down(x):
        ahead, behind = next_in(x, 0), last_in(x, 0)
        swapped = pltpu.roll(jnp.where(front, ahead, behind), 64, 1)
        return jnp.where(even, ahead, swapped), jnp.where(even, swapped, behind)

    k_coarse(-1, s.far_recv)
    half = 0.5 * 0.0625
    reach = low_cols * REACH
    for a in range(1, 2 * reach + low_cols - 1):
        k = s.k2[a]
        above, below = up_and_down(k)
        above = half * (k + jnp.where(top, 0.0, above))
        below = half * (k + jnp.where(bottom, 0.0, below))
        up = half * (k + s.k2[a + 1])
        down = half * (k + s.k2[a - 1])
        out = half * (k + jnp.where(inner_last, 0.0, next_in(k, 1)))
        back = jnp.where(inner_first, half * k, last_in(out, 1))
        s.inv2[a] = 1.0 / (shift_value + (up + down + above + below + out + back))
        s.up2[a] = up
        s.above2[a] = jnp.where(top, 0.0, above)
        s.below2[a] = jnp.where(bottom, 0.0, below)
        s.out2[a] = jnp.where(inner_last, 0.0, out)

    b_coarse(-1, s.far_recv)
    first, steps = chebyshev_steps(COARSE_SWEEPS, coarse_low)
    size = 2 * reach + low_cols
    x = [None] + [s.b2[a] * s.inv2[a] * first for a in range(1, size - 1)] + [None]
    before = [None] * size
    for number, (scale, keep, add) in enumerate(steps):
        new = [None] * size
        for a in range(number + 2, size - number - 2):
            above, below = up_and_down(x[a])
            total = s.b2[a] + s.up2[a] * x[a + 1] + s.up2[a - 1] * x[a - 1]
            total = total + (s.above2[a] * above + s.below2[a] * below)
            out = s.out2[a]
            total = total + (out * next_in(x[a], 1) + last_in(out * x[a], 1))
            new[a] = scale * x[a] + add * (total * s.inv2[a])
            if number:
                new[a] = new[a] - keep * before[a]
        x, before = new, x

    tiles = []
    for i in range(low_cols):
        mine = pltpu.roll(x[reach + i], lax.rem(2 * n_ht - 2 * ht, 2 * n_ht), 0)
        mine = jnp.where(sub < 4, mine[0:1], mine[1:2])
        tiles += [mine, pltpu.roll(mine, 64, 1)]
    raised = exact_dot(jnp.concatenate(tiles, axis=0), s.wide1[...])
    for a in range(cols):
        res[a] = res[a] + raised[rows * (a // 4) : rows * (a // 4) + rows]

    grouped(sent, lambda copy: copy.wait_send())
    k_coarse(1, s.far_send)
    b_coarse(1, s.far_send)


class Scratch:
    pass


def scratch_shapes(cols, rows, lanes, n_ht):
    mid_cols, mid_rows, mid_lanes = cols // 2, rows // 2, lanes // 2
    low_cols = mid_cols // 2
    fields = {
        "coef": (cols, rows, lanes),
        "halves": (mid_cols * rows, mid_lanes),
        "doubled": (mid_cols * rows, mid_lanes),
        "kept_k": (low_cols, 8, 128),
        "kept_b": (low_cols, 8, 128),
        "tally": ((2 * REACH + 1) * low_cols, 2, 128),
    }
    for level, (size, sub, width) in enumerate([(cols, rows + 8, lanes), (mid_cols, mid_rows + 8, mid_lanes)]):
        fields[f"k{level}"] = (size + 10, sub + 8, width)
        for name in ("b", "x", "y", "up", "side", "out", "inv", "piv"):
            fields[f"{name}{level}"] = (size + 8, sub, width)
    for name in ("k2", "b2", "up2", "above2", "below2", "out2", "inv2"):
        fields[name] = ((2 * REACH + 1) * low_cols, 2 * n_ht, 128)
    shapes = {name: pltpu.VMEM(shape, F32) for name, shape in fields.items()}
    shapes["kind"] = pltpu.VMEM((cols, rows, lanes), jnp.int32)
    shapes["down0"] = pltpu.VMEM((lanes, mid_lanes), BF16)
    shapes["down1"] = pltpu.VMEM((mid_lanes, 128), BF16)
    shapes["wide0"] = pltpu.VMEM((mid_lanes, lanes), BF16)
    shapes["wide1"] = pltpu.VMEM((128, lanes), BF16)
    shapes["load_sem"] = pltpu.SemaphoreType.DMA((3,))
    shapes["send_sem"] = pltpu.SemaphoreType.DMA((32,))
    shapes["recv_sem"] = pltpu.SemaphoreType.DMA((32,))
    shapes["own_sem"] = pltpu.SemaphoreType.DMA((2,))
    shapes["ready"] = pltpu.SemaphoreType.REGULAR
    shapes["far_send"] = pltpu.SemaphoreType.DMA((10,))
    shapes["far_recv"] = pltpu.SemaphoreType.DMA((10,))
    return shapes


def solution(mesh):
    n_ht, n_az = mesh.shape["ht"], mesh.shape["az"]

    def on_device(right_side, base_coef, cell_type):
        blocks = [jnp.transpose(block, (1, 0, 2)) for block in (right_side, base_coef, cell_type)]
        shape = blocks[0].shape
        shapes = scratch_shapes(*shape, n_ht)

        def body(rhs, coef, kind, res, *refs):
            s = Scratch()
            for name, ref in zip(shapes, refs):
                setattr(s, name, ref)
            kernel(n_ht, n_az, rhs, coef, kind, res, s)

        result = pl.pallas_call(
            body,
            out_shape=pltpu.VMEM(shape, F32),
            in_specs=[pl.BlockSpec(memory_space=pltpu.HBM)] * 3,
            out_specs=pl.BlockSpec(memory_space=pltpu.VMEM),
            scratch_shapes=list(shapes.values()),
            compiler_params=pltpu.CompilerParams(
                collective_id=0, has_side_effects=True, vmem_limit_bytes=56 * 1024 * 1024
            ),
        )(*blocks)
        return jnp.transpose(result, (1, 0, 2))

    placed = P("ht", "az", None)
    return jax.shard_map(
        on_device, mesh=mesh, in_specs=(placed,) * 3, out_specs=placed, check_vma=False
    )
```

```python
import jax
import jax.numpy as jnp
from jax import lax
from jax.experimental import pallas as pl
from jax.experimental.pallas import tpu as pltpu
from jax.sharding import PartitionSpec as P

DEGREE = 4
COARSE_SWEEPS = 6

shift_value = 0.002
smooth_low = 0.3
coarse_low = 0.02
high_end = 2.0

F32 = jnp.float32
BF16 = jnp.bfloat16
MESH = pl.DeviceIdType.MESH

SIDES = [(0, 1), (0, -1)]
ENDS = [(1, 0), (-1, 0)]
CORNERS = [(1, 1), (1, -1), (-1, 1), (-1, -1)]
NEAR = SIDES + ENDS + CORNERS
REACH = 2


def chebyshev_steps(degree, low_end):
    middle = 0.5 * (high_end + low_end)
    spread = 0.5 * (high_end - low_end)
    sigma_ratio = middle / spread
    rho_now = 1.0 / sigma_ratio
    steps = []
    for _ in range(degree - 1):
        rho_next = 1.0 / (2.0 * sigma_ratio - rho_now)
        keep, add = rho_next * rho_now, 2.0 * rho_next / spread
        steps.append((1.0 + keep - add, keep, add))
        rho_now = rho_next
    return 1.0 / middle, steps


def exact_dot(values, weights):
    count = values.shape[0]
    high = values.astype(BF16)
    rest = values - high.astype(F32)
    mid = rest.astype(BF16)
    low = (rest - mid.astype(F32)).astype(BF16)
    pieces = jnp.concatenate([high, mid, low], axis=0)
    total = jnp.dot(pieces, weights, preferred_element_type=F32)
    return total[0:count] + total[count : 2 * count] + total[2 * count :]


def each_row(ranges, body):
    for first, count, block in ranges:
        if block >= count:
            for i in range(count):
                body(first + i)
            continue

        def step(i, carry, first=first, block=block):
            for j in range(block):
                body(first + i * block + j)
            return carry

        lax.fori_loop(0, count // block, step, 0)


def next_in(values, axis):
    return pltpu.roll(values, values.shape[axis] - 1, axis)


def last_in(values, axis):
    return pltpu.roll(values, 1, axis)


def iotas(shape):
    return lax.broadcasted_iota(jnp.int32, shape, 0), lax.broadcasted_iota(jnp.int32, shape, 1)


class Level:
    def __init__(self, s, level, own, spacing, low_end, degree):
        for name in ("k", "b", "x", "y", "up", "side", "out", "inv", "piv"):
            setattr(self, name, getattr(s, f"{name}{level}"))
        self.own_az, self.own_ht = own
        self.rows, self.sub, self.lanes = self.b.shape
        self.half = 0.5 * spacing
        self.first, self.steps = chebyshev_steps(degree, low_end)

    def clear(self):
        for field in (self.k, self.b):
            rest = field.at[:, self.own_ht :]
            rest[...] = jnp.zeros(rest.shape, F32)

    def set_up(self, ranges, below, above):
        sub, lane = iotas((self.sub, self.lanes))
        last_lane, first_lane = lane == self.lanes - 1, lane == 0
        top, bottom = sub == self.own_ht + 3, sub == self.own_ht + 4
        lost = ((sub >= self.own_ht) & (sub < self.own_ht + 4) & jnp.logical_not(above)) | (
            (sub >= self.own_ht + 4) & jnp.logical_not(below)
        )
        inside = jnp.where(lost, 0.0, 1.0).astype(F32)

        own, nearer = self.own_ht, iotas((8, self.lanes))[0] < 4

        def folded(i):
            halo = jnp.where(nearer, self.k[i, own : own + 8], self.k[i, own + 8 : own + 16])
            return jnp.concatenate([self.k[i, 0:own], halo], axis=0)

        def body(i):
            k = folded(i + 1)
            up = self.half * (k + folded(i + 2))
            down = self.half * (k + folded(i))
            fifth_up, fifth_down = self.k[i + 1, own + 4 : own + 5], self.k[i + 1, own + 11 : own + 12]
            side = self.half * (k + jnp.where(top, fifth_up, next_in(k, 0)))
            under = jnp.where(bottom, self.half * (k + fifth_down), last_in(side, 0))
            out = self.half * (k + jnp.where(last_lane, 0.0, next_in(k, 1)))
            back = jnp.where(first_lane, self.half * k, last_in(out, 1))
            piv = shift_value + (up + down + side + under + out + back)
            self.up[i], self.side[i], self.piv[i] = up, side, piv
            self.out[i] = jnp.where(last_lane, 0.0, out)
            self.inv[i] = inside / piv

        each_row(ranges, body)

    def gathered(self, field, i):
        x, side, out = field[i], self.side[i], self.out[i]
        total = self.b[i] + self.up[i] * field[i + 1] + self.up[i - 1] * field[i - 1]
        total = total + (side * next_in(x, 0) + last_in(side * x, 0))
        return total + (out * next_in(x, 1) + last_in(out * x, 1)), x

    def start(self, ranges):
        def body(i):
            self.x[i] = self.b[i] * self.inv[i] * self.first

        each_row(ranges, body)

    def sweep(self, number, ranges):
        scale, keep, add = self.steps[number]
        old, new = self.fields(number)

        def body(i):
            total, x = self.gathered(old, i)
            value = scale * x + add * (total * self.inv[i])
            new[i] = value - keep * new[i] if number else value

        each_row(ranges, body)

    def fields(self, number):
        return (self.y, self.x) if number % 2 else (self.x, self.y)

    def result(self):
        return self.fields(len(self.steps))[0]

    def residual(self, i):
        total, x = self.gathered(self.result(), i)
        return total - self.piv[i] * x


def span(step, layers, halo, own, here):
    if step == 0:
        return pl.ds(halo, own)
    if step == 1:
        return pl.ds(halo + own - layers if here else halo - layers, layers)
    return pl.ds(halo if here else halo + own, layers)


def span_up(step, layers, sub, own, here):
    if step == 0:
        return pl.ds(0, own)
    if step == 1:
        return pl.ds(own - layers if here else sub - layers, layers)
    return pl.ds(0 if here else own, layers)


def kernel(n_ht, n_az, rhs_hbm, coef_hbm, type_hbm, res, s):
    ht, az = lax.axis_index("ht"), lax.axis_index("az")
    has = {1: ht < n_ht - 1, -1: ht > 0}
    cols, rows, _ = rhs_hbm.shape
    mid_cols, mid_rows = cols // 2, rows // 2
    low_cols = mid_cols // 2
    fine = Level(s, 0, (cols, rows), 1.0, smooth_low, DEGREE)
    middle = Level(s, 1, (mid_cols, mid_rows), 0.25, smooth_low, DEGREE)

    def there(dh, run):
        if dh == 0:
            run()
        else:
            pl.when(has[dh])(run)

    @pl.when(jnp.logical_not(has[1] & has[-1]))
    def _():
        fine.clear()
        middle.clear()

    s.k2[...] = jnp.zeros_like(s.k2)
    s.b2[...] = jnp.zeros_like(s.b2)

    def device(dh, da):
        return {"ht": ht + dh, "az": lax.rem(az + (da + n_az), n_az)}

    def grouped(copies, act):
        for dh in (1, -1, 0):
            group = [copy for step, copy in copies if step == dh]

            def run(group=group):
                for copy in group:
                    act(copy)

            there(dh, run)

    barrier = pltpu.get_barrier_semaphore()
    grouped(
        [(dh, (dh, da)) for dh, da in ENDS + SIDES],
        lambda step: pl.semaphore_signal(barrier, inc=1, device_id=device(*step), device_id_type=MESH),
    )
    loads = [
        pltpu.make_async_copy(coef_hbm, s.coef, s.load_sem.at[0]),
        pltpu.make_async_copy(type_hbm, s.kind, s.load_sem.at[1]),
        pltpu.make_async_copy(rhs_hbm, s.b0.at[pl.ds(4, cols), pl.ds(0, rows)], s.load_sem.at[2]),
    ]
    for load in loads:
        load.start()

    sent = []

    def exchange(slot, directions, field, level, halo, layers):
        made = []
        for dh, da in directions:

            def part(here):
                return field.at[
                    span(da, layers, halo, level.own_az, here),
                    span_up(dh, layers, field.shape[1], level.own_ht, here),
                ]

            number = slot + NEAR.index((dh, da))
            copy = pltpu.make_async_remote_copy(
                src_ref=part(True),
                dst_ref=part(False),
                send_sem=s.send_sem.at[number],
                recv_sem=s.recv_sem.at[number],
                device_id=device(dh, da),
                device_id_type=MESH,
            )
            made.append((dh, copy))
        grouped(made, lambda copy: copy.start())
        sent.extend(made)
        return made

    def arrived(made):
        grouped([(-dh, copy) for dh, copy in made], lambda copy: copy.wait_recv())

    loads[0].wait()
    loads[1].wait()

    def conductivity(a):
        kind = s.kind[a]
        factor = jnp.where(kind == 0, 0.1, jnp.where(kind == 1, 0.4, 1.0)).astype(F32)
        s.k0[5 + a, 0:rows] = s.coef[a] * factor

    each_row([(0, cols, 6)], conductivity)
    ends = jnp.where(has[1], 1, 0) + jnp.where(has[-1], 1, 0)
    pl.semaphore_wait(barrier, 2 + ends)
    grouped(
        [(dh, (dh, da)) for dh, da in ENDS],
        lambda step: pl.semaphore_signal(s.ready, inc=1, device_id=device(*step), device_id_type=MESH),
    )
    k_sides = exchange(0, SIDES, s.k0, fine, 5, 5)
    k_ends = exchange(0, ENDS, s.k0, fine, 5, 5)
    loads[2].wait()
    b_ends = exchange(8, ENDS, s.b0, fine, 4, 4)
    pl.semaphore_wait(s.ready, ends)
    k_sides += exchange(0, CORNERS, s.k0, fine, 5, 4)
    b_sides = exchange(8, CORNERS, s.b0, fine, 4, 3)
    b_sides += exchange(8, SIDES, s.b0, fine, 4, 4)

    def as_weights(picked, value):
        return jnp.where(picked, value, 0.0).astype(BF16)

    i, j = iotas(s.down0.shape)
    s.down0[...] = as_weights(i // 2 == j, 0.125)
    i, j = iotas(s.down1.shape)
    s.down1[...] = as_weights(i // 2 == j % 64, 0.125)
    i, j = iotas(s.wide0.shape)
    s.wide0[...] = as_weights(i == j // 2, 1.0)
    i, j = iotas(s.wide1.shape)
    s.wide1[...] = as_weights(i == j // 4, 1.0)

    sub, lane = iotas((8, 128))
    front = lane < 64
    even = sub % 2 == 0

    def restrict0(pair):
        pairs = jnp.concatenate([pair(i) for i in range(mid_cols)], axis=0)
        s.halves[...] = exact_dot(pairs, s.down0[...])
        count = mid_cols * mid_rows
        means = s.halves[pl.ds(0, count, stride=2), :] + s.halves[pl.ds(1, count, stride=2), :]
        return means.reshape(mid_cols, mid_rows, -1)

    def restrict1(pair):
        sums = exact_dot(jnp.concatenate([pair(i) for i in range(low_cols)], axis=0), s.down1[...])
        packed = []
        for i in range(low_cols):
            mean = sums[8 * i : 8 * i + 8]
            mean = mean + next_in(mean, 0)
            mean = jnp.where(front, mean, pltpu.roll(mean, 4, 0))
            packed.append(jnp.where(sub == 1, next_in(mean, 0), mean))
        return packed

    def spread(kept, field, first, groups):
        block = kept.at[:, pl.ds(0, 2)]

        def there_far(dh, run):
            if abs(dh) < 2:
                there(dh, run)
            else:
                pl.when((ht + dh >= 0) & (ht + dh < n_ht))(run)

        def place(da):
            return field.at[pl.ds((REACH - da) * low_cols, low_cols), pl.ds(2 * ht, 2)]

        for number, (dh, reached) in enumerate(groups, first):

            def go(dh=dh, reached=reached, number=number):
                for da in reached:
                    pltpu.make_async_remote_copy(
                        src_ref=block,
                        dst_ref=place(da),
                        send_sem=s.far_send.at[number],
                        recv_sem=s.far_recv.at[number],
                        device_id=device(dh, da),
                        device_id_type=MESH,
                    ).start()

            there_far(dh, go)
        own = pltpu.make_async_copy(block, place(0), s.own_sem.at[first // len(groups)])
        own.start()

        def finish(towards, sems):
            for number, (dh, reached) in enumerate(groups, first):
                some = s.tally.at[pl.ds(0, len(reached) * low_cols)]

                def wait(number=number, some=some):
                    pltpu.make_async_copy(some, some, sems.at[number]).wait()

                there_far(towards * dh, wait)
            if towards < 0:
                own.wait()

        return finish

    kappa1 = restrict0(lambda i: s.k0[5 + 2 * i, 0:rows] + s.k0[6 + 2 * i, 0:rows])
    s.k1[5 : 5 + mid_cols, 0:mid_rows] = kappa1
    kappa2 = restrict1(lambda i: kappa1[2 * i] + kappa1[2 * i + 1])
    for i, block in enumerate(kappa2):
        s.kept_k[i] = block

    last = fine.rows
    arrived(k_ends)
    fine.set_up([(5, cols - 2, 10)], has[-1], has[1])
    arrived(k_sides)
    fine.set_up([(0, 5, 5), (last - 5, 5, 5)], has[-1], has[1])
    arrived(b_ends)
    fine.start([(4, cols, 12)])
    for number, block in enumerate((10, 8, 6)):
        fine.sweep(number, [(5 + number, cols - 2 - 2 * number, block)])
    k_middle = exchange(16, CORNERS, s.k1, middle, 5, 4)
    k_middle += exchange(16, ENDS + SIDES, s.k1, middle, 5, 5)
    arrived(b_sides)
    fine.start([(0, 4, 4), (last - 4, 4, 4)])
    for number in range(len(fine.steps)):
        fine.sweep(number, [(1 + number, 4, 4), (last - 5 - number, 4, 4)])

    r0 = [fine.residual(4 + i)[0:rows] for i in range(cols)]
    s.b1[4 : 4 + mid_cols, 0:mid_rows] = restrict0(lambda i: r0[2 * i] + r0[2 * i + 1])
    b_middle = exchange(24, CORNERS, s.b1, middle, 4, 3)
    b_near = exchange(24, ENDS, s.b1, middle, 4, 4)
    b_middle += exchange(24, SIDES, s.b1, middle, 4, 4)
    around = [2, -2, 1, -1]
    k_coarse = spread(s.kept_k, s.k2, 0, [(1, around + [0]), (-1, around + [0]), (2, [1, -1, 0]), (-2, [1, -1, 0]), (0, around)])

    arrived(k_middle)
    middle.set_up([(0, middle.rows, 7)], has[-1], has[1])
    arrived(b_near + b_middle)
    middle.start([(0, middle.rows, middle.rows)])
    for number in range(len(middle.steps)):
        count = middle.rows - 2 - 2 * number
        middle.sweep(number, [(1 + number, count, count)])
    r1 = [middle.residual(4 + i)[0:mid_rows] for i in range(mid_cols)]
    for i, block in enumerate(restrict1(lambda i: r1[2 * i] + r1[2 * i + 1])):
        s.kept_b[i] = block
    b_coarse = spread(s.kept_b, s.b2, 5, [(1, around + [0]), (-1, around + [0]), (2, [0]), (-2, [0]), (0, around)])

    parts = middle.result()[4 : 4 + mid_cols, 0:mid_rows].reshape(mid_cols * mid_rows, -1)
    count = mid_cols * mid_rows
    s.doubled[pl.ds(0, count, stride=2), :] = parts
    s.doubled[pl.ds(1, count, stride=2), :] = parts
    raised = exact_dot(s.doubled[...], s.wide0[...])
    for a in range(cols):
        res[a] = fine.result()[4 + a, 0:rows] + raised[rows * (a // 2) : rows * (a // 2) + rows]

    inner_last, inner_first = lane % 64 == 63, lane % 64 == 0
    top = (sub == 2 * n_ht - 1) & jnp.logical_not(front)
    bottom = (sub == 0) & front

    def up_and_down(x):
        ahead, behind = next_in(x, 0), last_in(x, 0)
        swapped = pltpu.roll(jnp.where(front, ahead, behind), 64, 1)
        return jnp.where(even, ahead, swapped), jnp.where(even, swapped, behind)

    k_coarse(-1, s.far_recv)
    half = 0.5 * 0.0625
    reach = low_cols * REACH
    for a in range(1, 2 * reach + low_cols - 1):
        k = s.k2[a]
        above, below = up_and_down(k)
        above = half * (k + jnp.where(top, 0.0, above))
        below = half * (k + jnp.where(bottom, 0.0, below))
        up = half * (k + s.k2[a + 1])
        down = half * (k + s.k2[a - 1])
        out = half * (k + jnp.where(inner_last, 0.0, next_in(k, 1)))
        back = jnp.where(inner_first, half * k, last_in(out, 1))
        s.inv2[a] = 1.0 / (shift_value + (up + down + above + below + out + back))
        s.up2[a] = up
        s.above2[a] = jnp.where(top, 0.0, above)
        s.below2[a] = jnp.where(bottom, 0.0, below)
        s.out2[a] = jnp.where(inner_last, 0.0, out)

    b_coarse(-1, s.far_recv)
    first, steps = chebyshev_steps(COARSE_SWEEPS, coarse_low)
    size = 2 * reach + low_cols
    x = [None] + [s.b2[a] * s.inv2[a] * first for a in range(1, size - 1)] + [None]
    before = [None] * size
    for number, (scale, keep, add) in enumerate(steps):
        new = [None] * size
        for a in range(number + 2, size - number - 2):
            above, below = up_and_down(x[a])
            total = s.b2[a] + s.up2[a] * x[a + 1] + s.up2[a - 1] * x[a - 1]
            total = total + (s.above2[a] * above + s.below2[a] * below)
            out = s.out2[a]
            total = total + (out * next_in(x[a], 1) + last_in(out * x[a], 1))
            new[a] = scale * x[a] + add * (total * s.inv2[a])
            if number:
                new[a] = new[a] - keep * before[a]
        x, before = new, x

    tiles = []
    for i in range(low_cols):
        mine = pltpu.roll(x[reach + i], lax.rem(2 * n_ht - 2 * ht, 2 * n_ht), 0)
        mine = jnp.where(sub < 4, mine[0:1], mine[1:2])
        tiles += [mine, pltpu.roll(mine, 64, 1)]
    raised = exact_dot(jnp.concatenate(tiles, axis=0), s.wide1[...])
    for a in range(cols):
        res[a] = res[a] + raised[rows * (a // 4) : rows * (a // 4) + rows]

    grouped(sent, lambda copy: copy.wait_send())
    k_coarse(1, s.far_send)
    b_coarse(1, s.far_send)


class Scratch:
    pass


def scratch_shapes(cols, rows, lanes, n_ht):
    mid_cols, mid_rows, mid_lanes = cols // 2, rows // 2, lanes // 2
    low_cols = mid_cols // 2
    fields = {
        "coef": (cols, rows, lanes),
        "halves": (mid_cols * rows, mid_lanes),
        "doubled": (mid_cols * rows, mid_lanes),
        "kept_k": (low_cols, 8, 128),
        "kept_b": (low_cols, 8, 128),
        "tally": ((2 * REACH + 1) * low_cols, 2, 128),
    }
    for level, (size, sub, width) in enumerate([(cols, rows + 8, lanes), (mid_cols, mid_rows + 8, mid_lanes)]):
        fields[f"k{level}"] = (size + 10, sub + 8, width)
        for name in ("b", "x", "y", "up", "side", "out", "inv", "piv"):
            fields[f"{name}{level}"] = (size + 8, sub, width)
    for name in ("k2", "b2", "up2", "above2", "below2", "out2", "inv2"):
        fields[name] = ((2 * REACH + 1) * low_cols, 2 * n_ht, 128)
    shapes = {name: pltpu.VMEM(shape, F32) for name, shape in fields.items()}
    shapes["kind"] = pltpu.VMEM((cols, rows, lanes), jnp.int32)
    shapes["down0"] = pltpu.VMEM((lanes, mid_lanes), BF16)
    shapes["down1"] = pltpu.VMEM((mid_lanes, 128), BF16)
    shapes["wide0"] = pltpu.VMEM((mid_lanes, lanes), BF16)
    shapes["wide1"] = pltpu.VMEM((128, lanes), BF16)
    shapes["load_sem"] = pltpu.SemaphoreType.DMA((3,))
    shapes["send_sem"] = pltpu.SemaphoreType.DMA((32,))
    shapes["recv_sem"] = pltpu.SemaphoreType.DMA((32,))
    shapes["own_sem"] = pltpu.SemaphoreType.DMA((2,))
    shapes["ready"] = pltpu.SemaphoreType.REGULAR
    shapes["far_send"] = pltpu.SemaphoreType.DMA((10,))
    shapes["far_recv"] = pltpu.SemaphoreType.DMA((10,))
    return shapes


def solution(mesh):
    n_ht, n_az = mesh.shape["ht"], mesh.shape["az"]

    def on_device(right_side, base_coef, cell_type):
        blocks = [jnp.transpose(block, (1, 0, 2)) for block in (right_side, base_coef, cell_type)]
        shape = blocks[0].shape
        shapes = scratch_shapes(*shape, n_ht)

        def body(rhs, coef, kind, res, *refs):
            s = Scratch()
            for name, ref in zip(shapes, refs):
                setattr(s, name, ref)
            kernel(n_ht, n_az, rhs, coef, kind, res, s)

        result = pl.pallas_call(
            body,
            out_shape=pltpu.VMEM(shape, F32),
            in_specs=[pl.BlockSpec(memory_space=pltpu.HBM)] * 3,
            out_specs=pl.BlockSpec(memory_space=pltpu.VMEM),
            scratch_shapes=list(shapes.values()),
            compiler_params=pltpu.CompilerParams(
                collective_id=0, has_side_effects=True, vmem_limit_bytes=56 * 1024 * 1024
            ),
        )(*blocks)
        return jnp.transpose(result, (1, 0, 2))

    placed = P("ht", "az", None)
    return jax.shard_map(
        on_device, mesh=mesh, in_specs=(placed,) * 3, out_specs=placed, check_vma=False
    )
```

```python
import jax
import jax.numpy as jnp
from jax import lax
from jax.experimental import pallas as pl
from jax.experimental.pallas import tpu as pltpu
from jax.sharding import PartitionSpec as P

DEGREE = 4
COARSE_SWEEPS = 6

shift_value = 0.002
smooth_low = 0.3
coarse_low = 0.02
high_end = 2.0

F32 = jnp.float32
BF16 = jnp.bfloat16
MESH = pl.DeviceIdType.MESH

SIDES = [(0, 1), (0, -1)]
ENDS = [(1, 0), (-1, 0)]
CORNERS = [(1, 1), (1, -1), (-1, 1), (-1, -1)]
NEAR = SIDES + ENDS + CORNERS
REACH = 2


def chebyshev_steps(degree, low_end):
    middle = 0.5 * (high_end + low_end)
    spread = 0.5 * (high_end - low_end)
    sigma_ratio = middle / spread
    rho_now = 1.0 / sigma_ratio
    steps = []
    for _ in range(degree - 1):
        rho_next = 1.0 / (2.0 * sigma_ratio - rho_now)
        keep, add = rho_next * rho_now, 2.0 * rho_next / spread
        steps.append((1.0 + keep - add, keep, add))
        rho_now = rho_next
    return 1.0 / middle, steps


def exact_dot(values, weights):
    count = values.shape[0]
    high = values.astype(BF16)
    rest = values - high.astype(F32)
    mid = rest.astype(BF16)
    low = (rest - mid.astype(F32)).astype(BF16)
    pieces = jnp.concatenate([high, mid, low], axis=0)
    total = jnp.dot(pieces, weights, preferred_element_type=F32)
    return total[0:count] + total[count : 2 * count] + total[2 * count :]


def each_row(ranges, body):
    for first, count, block in ranges:
        if block >= count:
            for i in range(count):
                body(first + i)
            continue

        def step(i, carry, first=first, block=block):
            for j in range(block):
                body(first + i * block + j)
            return carry

        lax.fori_loop(0, count // block, step, 0)


def next_in(values, axis):
    return pltpu.roll(values, values.shape[axis] - 1, axis)


def last_in(values, axis):
    return pltpu.roll(values, 1, axis)


def iotas(shape):
    return lax.broadcasted_iota(jnp.int32, shape, 0), lax.broadcasted_iota(jnp.int32, shape, 1)


class Level:
    def __init__(self, s, level, own, spacing, low_end, degree):
        for name in ("k", "b", "x", "y", "up", "side", "out", "inv", "piv"):
            setattr(self, name, getattr(s, f"{name}{level}"))
        self.own_az, self.own_ht = own
        self.rows, self.sub, self.lanes = self.b.shape
        self.half = 0.5 * spacing
        self.first, self.steps = chebyshev_steps(degree, low_end)

    def clear(self):
        for field in (self.k, self.b):
            rest = field.at[:, self.own_ht :]
            rest[...] = jnp.zeros(rest.shape, F32)

    def set_up(self, ranges, below, above):
        sub, lane = iotas((self.sub, self.lanes))
        last_lane, first_lane = lane == self.lanes - 1, lane == 0
        top, bottom = sub == self.own_ht + 3, sub == self.own_ht + 4
        lost = ((sub >= self.own_ht) & (sub < self.own_ht + 4) & jnp.logical_not(above)) | (
            (sub >= self.own_ht + 4) & jnp.logical_not(below)
        )
        inside = jnp.where(lost, 0.0, 1.0).astype(F32)

        own, nearer = self.own_ht, iotas((8, self.lanes))[0] < 4

        def folded(i):
            halo = jnp.where(nearer, self.k[i, own : own + 8], self.k[i, own + 8 : own + 16])
            return jnp.concatenate([self.k[i, 0:own], halo], axis=0)

        def body(i):
            k = folded(i + 1)
            up = self.half * (k + folded(i + 2))
            down = self.half * (k + folded(i))
            fifth_up, fifth_down = self.k[i + 1, own + 4 : own + 5], self.k[i + 1, own + 11 : own + 12]
            side = self.half * (k + jnp.where(top, fifth_up, next_in(k, 0)))
            under = jnp.where(bottom, self.half * (k + fifth_down), last_in(side, 0))
            out = self.half * (k + jnp.where(last_lane, 0.0, next_in(k, 1)))
            back = jnp.where(first_lane, self.half * k, last_in(out, 1))
            piv = shift_value + (up + down + side + under + out + back)
            self.up[i], self.side[i], self.piv[i] = up, side, piv
            self.out[i] = jnp.where(last_lane, 0.0, out)
            self.inv[i] = inside / piv

        each_row(ranges, body)

    def gathered(self, field, i):
        x, side, out = field[i], self.side[i], self.out[i]
        total = self.b[i] + self.up[i] * field[i + 1] + self.up[i - 1] * field[i - 1]
        total = total + (side * next_in(x, 0) + last_in(side * x, 0))
        return total + (out * next_in(x, 1) + last_in(out * x, 1)), x

    def start(self, ranges):
        def body(i):
            self.x[i] = self.b[i] * self.inv[i] * self.first

        each_row(ranges, body)

    def sweep(self, number, ranges):
        scale, keep, add = self.steps[number]
        old, new = self.fields(number)

        def body(i):
            total, x = self.gathered(old, i)
            value = scale * x + add * (total * self.inv[i])
            new[i] = value - keep * new[i] if number else value

        each_row(ranges, body)

    def fields(self, number):
        return (self.y, self.x) if number % 2 else (self.x, self.y)

    def result(self):
        return self.fields(len(self.steps))[0]

    def residual(self, i):
        total, x = self.gathered(self.result(), i)
        return total - self.piv[i] * x


def span(step, layers, halo, own, here):
    if step == 0:
        return pl.ds(halo, own)
    if step == 1:
        return pl.ds(halo + own - layers if here else halo - layers, layers)
    return pl.ds(halo if here else halo + own, layers)


def span_up(step, layers, sub, own, here):
    if step == 0:
        return pl.ds(0, own)
    if step == 1:
        return pl.ds(own - layers if here else sub - layers, layers)
    return pl.ds(0 if here else own, layers)


def kernel(n_ht, n_az, rhs_hbm, coef_hbm, type_hbm, res, s):
    ht, az = lax.axis_index("ht"), lax.axis_index("az")
    has = {1: ht < n_ht - 1, -1: ht > 0}
    cols, rows, _ = rhs_hbm.shape
    mid_cols, mid_rows = cols // 2, rows // 2
    low_cols = mid_cols // 2
    fine = Level(s, 0, (cols, rows), 1.0, smooth_low, DEGREE)
    middle = Level(s, 1, (mid_cols, mid_rows), 0.25, smooth_low, DEGREE)

    def there(dh, run):
        if dh == 0:
            run()
        else:
            pl.when(has[dh])(run)

    @pl.when(jnp.logical_not(has[1] & has[-1]))
    def _():
        fine.clear()
        middle.clear()

    s.k2[...] = jnp.zeros_like(s.k2)
    s.b2[...] = jnp.zeros_like(s.b2)

    def device(dh, da):
        return {"ht": ht + dh, "az": lax.rem(az + (da + n_az), n_az)}

    def grouped(copies, act):
        for dh in (1, -1, 0):
            group = [copy for step, copy in copies if step == dh]

            def run(group=group):
                for copy in group:
                    act(copy)

            there(dh, run)

    barrier = pltpu.get_barrier_semaphore()
    grouped(
        [(dh, (dh, da)) for dh, da in ENDS + SIDES],
        lambda step: pl.semaphore_signal(barrier, inc=1, device_id=device(*step), device_id_type=MESH),
    )
    loads = [
        pltpu.make_async_copy(coef_hbm, s.coef, s.load_sem.at[0]),
        pltpu.make_async_copy(type_hbm, s.kind, s.load_sem.at[1]),
        pltpu.make_async_copy(rhs_hbm, s.b0.at[pl.ds(4, cols), pl.ds(0, rows)], s.load_sem.at[2]),
    ]
    for load in loads:
        load.start()

    sent = []

    def exchange(slot, directions, field, level, halo, layers):
        made = []
        for dh, da in directions:

            def part(here):
                return field.at[
                    span(da, layers, halo, level.own_az, here),
                    span_up(dh, layers, field.shape[1], level.own_ht, here),
                ]

            number = slot + NEAR.index((dh, da))
            copy = pltpu.make_async_remote_copy(
                src_ref=part(True),
                dst_ref=part(False),
                send_sem=s.send_sem.at[number],
                recv_sem=s.recv_sem.at[number],
                device_id=device(dh, da),
                device_id_type=MESH,
            )
            made.append((dh, copy))
        grouped(made, lambda copy: copy.start())
        sent.extend(made)
        return made

    def arrived(made):
        grouped([(-dh, copy) for dh, copy in made], lambda copy: copy.wait_recv())

    loads[0].wait()
    loads[1].wait()

    def conductivity(a):
        kind = s.kind[a]
        factor = jnp.where(kind == 0, 0.1, jnp.where(kind == 1, 0.4, 1.0)).astype(F32)
        s.k0[5 + a, 0:rows] = s.coef[a] * factor

    each_row([(0, cols, 6)], conductivity)
    ends = jnp.where(has[1], 1, 0) + jnp.where(has[-1], 1, 0)
    pl.semaphore_wait(barrier, 2 + ends)
    grouped(
        [(dh, (dh, da)) for dh, da in ENDS],
        lambda step: pl.semaphore_signal(s.ready, inc=1, device_id=device(*step), device_id_type=MESH),
    )
    k_sides = exchange(0, SIDES, s.k0, fine, 5, 5)
    k_ends = exchange(0, ENDS, s.k0, fine, 5, 5)
    loads[2].wait()
    pl.semaphore_wait(s.ready, ends)
    k_sides += exchange(0, CORNERS, s.k0, fine, 5, 4)
    b_sides = exchange(8, CORNERS, s.b0, fine, 4, 3)
    b_ends = exchange(8, ENDS, s.b0, fine, 4, 4)
    b_sides += exchange(8, SIDES, s.b0, fine, 4, 4)

    def as_weights(picked, value):
        return jnp.where(picked, value, 0.0).astype(BF16)

    i, j = iotas(s.down0.shape)
    s.down0[...] = as_weights(i // 2 == j, 0.125)
    i, j = iotas(s.down1.shape)
    s.down1[...] = as_weights(i // 2 == j % 64, 0.125)
    i, j = iotas(s.wide0.shape)
    s.wide0[...] = as_weights(i == j // 2, 1.0)
    i, j = iotas(s.wide1.shape)
    s.wide1[...] = as_weights(i == j // 4, 1.0)

    sub, lane = iotas((8, 128))
    front = lane < 64
    even = sub % 2 == 0

    def restrict0(pair):
        pairs = jnp.concatenate([pair(i) for i in range(mid_cols)], axis=0)
        s.halves[...] = exact_dot(pairs, s.down0[...])
        count = mid_cols * mid_rows
        means = s.halves[pl.ds(0, count, stride=2), :] + s.halves[pl.ds(1, count, stride=2), :]
        return means.reshape(mid_cols, mid_rows, -1)

    def restrict1(pair):
        sums = exact_dot(jnp.concatenate([pair(i) for i in range(low_cols)], axis=0), s.down1[...])
        packed = []
        for i in range(low_cols):
            mean = sums[8 * i : 8 * i + 8]
            mean = mean + next_in(mean, 0)
            mean = jnp.where(front, mean, pltpu.roll(mean, 4, 0))
            packed.append(jnp.where(sub == 1, next_in(mean, 0), mean))
        return packed

    def spread(kept, field, first, groups):
        block = kept.at[:, pl.ds(0, 2)]

        def there_far(dh, run):
            if abs(dh) < 2:
                there(dh, run)
            else:
                pl.when((ht + dh >= 0) & (ht + dh < n_ht))(run)

        def place(da):
            return field.at[pl.ds((REACH - da) * low_cols, low_cols), pl.ds(2 * ht, 2)]

        for number, (dh, reached) in enumerate(groups, first):

            def go(dh=dh, reached=reached, number=number):
                for da in reached:
                    pltpu.make_async_remote_copy(
                        src_ref=block,
                        dst_ref=place(da),
                        send_sem=s.far_send.at[number],
                        recv_sem=s.far_recv.at[number],
                        device_id=device(dh, da),
                        device_id_type=MESH,
                    ).start()

            there_far(dh, go)
        own = pltpu.make_async_copy(block, place(0), s.own_sem.at[first // len(groups)])
        own.start()

        def finish(towards, sems):
            for number, (dh, reached) in enumerate(groups, first):
                some = s.tally.at[pl.ds(0, len(reached) * low_cols)]

                def wait(number=number, some=some):
                    pltpu.make_async_copy(some, some, sems.at[number]).wait()

                there_far(towards * dh, wait)
            if towards < 0:
                own.wait()

        return finish

    kappa1 = restrict0(lambda i: s.k0[5 + 2 * i, 0:rows] + s.k0[6 + 2 * i, 0:rows])
    s.k1[5 : 5 + mid_cols, 0:mid_rows] = kappa1
    kappa2 = restrict1(lambda i: kappa1[2 * i] + kappa1[2 * i + 1])
    for i, block in enumerate(kappa2):
        s.kept_k[i] = block

    last = fine.rows
    arrived(k_ends)
    fine.set_up([(5, cols - 2, 10)], has[-1], has[1])
    arrived(k_sides)
    fine.set_up([(0, 5, 5), (last - 5, 5, 5)], has[-1], has[1])
    arrived(b_ends)
    fine.start([(4, cols, 12)])
    for number, block in enumerate((10, 8, 6)):
        fine.sweep(number, [(5 + number, cols - 2 - 2 * number, block)])
    k_middle = exchange(16, CORNERS, s.k1, middle, 5, 4)
    k_middle += exchange(16, ENDS + SIDES, s.k1, middle, 5, 5)
    arrived(b_sides)
    fine.start([(0, 4, 4), (last - 4, 4, 4)])
    for number in range(len(fine.steps)):
        fine.sweep(number, [(1 + number, 4, 4), (last - 5 - number, 4, 4)])

    r0 = [fine.residual(4 + i)[0:rows] for i in range(cols)]
    s.b1[4 : 4 + mid_cols, 0:mid_rows] = restrict0(lambda i: r0[2 * i] + r0[2 * i + 1])
    b_middle = exchange(24, CORNERS, s.b1, middle, 4, 3)
    b_near = exchange(24, ENDS, s.b1, middle, 4, 4)
    b_middle += exchange(24, SIDES, s.b1, middle, 4, 4)
    around = [2, -2, 1, -1]
    k_coarse = spread(s.kept_k, s.k2, 0, [(1, around + [0]), (-1, around + [0]), (2, [1, -1, 0]), (-2, [1, -1, 0]), (0, around)])

    arrived(k_middle)
    middle.set_up([(0, middle.rows, 7)], has[-1], has[1])
    arrived(b_near + b_middle)
    middle.start([(0, middle.rows, middle.rows)])
    for number in range(len(middle.steps)):
        count = middle.rows - 2 - 2 * number
        middle.sweep(number, [(1 + number, count, count)])
    r1 = [middle.residual(4 + i)[0:mid_rows] for i in range(mid_cols)]
    for i, block in enumerate(restrict1(lambda i: r1[2 * i] + r1[2 * i + 1])):
        s.kept_b[i] = block
    b_coarse = spread(s.kept_b, s.b2, 5, [(1, around + [0]), (-1, around + [0]), (2, [0]), (-2, [0]), (0, around)])

    parts = middle.result()[4 : 4 + mid_cols, 0:mid_rows].reshape(mid_cols * mid_rows, -1)
    count = mid_cols * mid_rows
    s.doubled[pl.ds(0, count, stride=2), :] = parts
    s.doubled[pl.ds(1, count, stride=2), :] = parts
    raised = exact_dot(s.doubled[...], s.wide0[...])
    for a in range(cols):
        res[a] = fine.result()[4 + a, 0:rows] + raised[rows * (a // 2) : rows * (a // 2) + rows]

    inner_last, inner_first = lane % 64 == 63, lane % 64 == 0
    top = (sub == 2 * n_ht - 1) & jnp.logical_not(front)
    bottom = (sub == 0) & front

    def up_and_down(x):
        ahead, behind = next_in(x, 0), last_in(x, 0)
        swapped = pltpu.roll(jnp.where(front, ahead, behind), 64, 1)
        return jnp.where(even, ahead, swapped), jnp.where(even, swapped, behind)

    k_coarse(-1, s.far_recv)
    half = 0.5 * 0.0625
    reach = low_cols * REACH
    for a in range(1, 2 * reach + low_cols - 1):
        k = s.k2[a]
        above, below = up_and_down(k)
        above = half * (k + jnp.where(top, 0.0, above))
        below = half * (k + jnp.where(bottom, 0.0, below))
        up = half * (k + s.k2[a + 1])
        down = half * (k + s.k2[a - 1])
        out = half * (k + jnp.where(inner_last, 0.0, next_in(k, 1)))
        back = jnp.where(inner_first, half * k, last_in(out, 1))
        s.inv2[a] = 1.0 / (shift_value + (up + down + above + below + out + back))
        s.up2[a] = up
        s.above2[a] = jnp.where(top, 0.0, above)
        s.below2[a] = jnp.where(bottom, 0.0, below)
        s.out2[a] = jnp.where(inner_last, 0.0, out)

    b_coarse(-1, s.far_recv)
    first, steps = chebyshev_steps(COARSE_SWEEPS, coarse_low)
    size = 2 * reach + low_cols
    x = [None] + [s.b2[a] * s.inv2[a] * first for a in range(1, size - 1)] + [None]
    before = [None] * size
    for number, (scale, keep, add) in enumerate(steps):
        new = [None] * size
        for a in range(number + 2, size - number - 2):
            above, below = up_and_down(x[a])
            total = s.b2[a] + s.up2[a] * x[a + 1] + s.up2[a - 1] * x[a - 1]
            total = total + (s.above2[a] * above + s.below2[a] * below)
            out = s.out2[a]
            total = total + (out * next_in(x[a], 1) + last_in(out * x[a], 1))
            new[a] = scale * x[a] + add * (total * s.inv2[a])
            if number:
                new[a] = new[a] - keep * before[a]
        x, before = new, x

    tiles = []
    for i in range(low_cols):
        mine = pltpu.roll(x[reach + i], lax.rem(2 * n_ht - 2 * ht, 2 * n_ht), 0)
        mine = jnp.where(sub < 4, mine[0:1], mine[1:2])
        tiles += [mine, pltpu.roll(mine, 64, 1)]
    raised = exact_dot(jnp.concatenate(tiles, axis=0), s.wide1[...])
    for a in range(cols):
        res[a] = res[a] + raised[rows * (a // 4) : rows * (a // 4) + rows]

    grouped(sent, lambda copy: copy.wait_send())
    k_coarse(1, s.far_send)
    b_coarse(1, s.far_send)


class Scratch:
    pass


def scratch_shapes(cols, rows, lanes, n_ht):
    mid_cols, mid_rows, mid_lanes = cols // 2, rows // 2, lanes // 2
    low_cols = mid_cols // 2
    fields = {
        "coef": (cols, rows, lanes),
        "halves": (mid_cols * rows, mid_lanes),
        "doubled": (mid_cols * rows, mid_lanes),
        "kept_k": (low_cols, 8, 128),
        "kept_b": (low_cols, 8, 128),
        "tally": ((2 * REACH + 1) * low_cols, 2, 128),
    }
    for level, (size, sub, width) in enumerate([(cols, rows + 8, lanes), (mid_cols, mid_rows + 8, mid_lanes)]):
        fields[f"k{level}"] = (size + 10, sub + 8, width)
        for name in ("b", "x", "y", "up", "side", "out", "inv", "piv"):
            fields[f"{name}{level}"] = (size + 8, sub, width)
    for name in ("k2", "b2", "up2", "above2", "below2", "out2", "inv2"):
        fields[name] = ((2 * REACH + 1) * low_cols, 2 * n_ht, 128)
    shapes = {name: pltpu.VMEM(shape, F32) for name, shape in fields.items()}
    shapes["kind"] = pltpu.VMEM((cols, rows, lanes), jnp.int32)
    shapes["down0"] = pltpu.VMEM((lanes, mid_lanes), BF16)
    shapes["down1"] = pltpu.VMEM((mid_lanes, 128), BF16)
    shapes["wide0"] = pltpu.VMEM((mid_lanes, lanes), BF16)
    shapes["wide1"] = pltpu.VMEM((128, lanes), BF16)
    shapes["load_sem"] = pltpu.SemaphoreType.DMA((3,))
    shapes["send_sem"] = pltpu.SemaphoreType.DMA((32,))
    shapes["recv_sem"] = pltpu.SemaphoreType.DMA((32,))
    shapes["own_sem"] = pltpu.SemaphoreType.DMA((2,))
    shapes["ready"] = pltpu.SemaphoreType.REGULAR
    shapes["far_send"] = pltpu.SemaphoreType.DMA((10,))
    shapes["far_recv"] = pltpu.SemaphoreType.DMA((10,))
    return shapes


def solution(mesh):
    n_ht, n_az = mesh.shape["ht"], mesh.shape["az"]

    def on_device(right_side, base_coef, cell_type):
        blocks = [jnp.transpose(block, (1, 0, 2)) for block in (right_side, base_coef, cell_type)]
        shape = blocks[0].shape
        shapes = scratch_shapes(*shape, n_ht)

        def body(rhs, coef, kind, res, *refs):
            s = Scratch()
            for name, ref in zip(shapes, refs):
                setattr(s, name, ref)
            kernel(n_ht, n_az, rhs, coef, kind, res, s)

        result = pl.pallas_call(
            body,
            out_shape=pltpu.VMEM(shape, F32),
            in_specs=[pl.BlockSpec(memory_space=pltpu.HBM)] * 3,
            out_specs=pl.BlockSpec(memory_space=pltpu.VMEM),
            scratch_shapes=list(shapes.values()),
            compiler_params=pltpu.CompilerParams(
                collective_id=0, has_side_effects=True, vmem_limit_bytes=56 * 1024 * 1024
            ),
        )(*blocks)
        return jnp.transpose(result, (1, 0, 2))

    placed = P("ht", "az", None)
    return jax.shard_map(
        on_device, mesh=mesh, in_specs=(placed,) * 3, out_specs=placed, check_vma=False
    )
```
